32 devices in a mesh: groups: 2 (over y), ctx: 4 (over z), head: 2 (over x), sub: 2 (over core).
Axes of the slice: x: 2, y: 2, z: 4, core: 2. Of those that a mesh axis runs over, the one named last changes fastest.
Arguments:
- tokens: bfloat16 [16384, 3584], P(('groups', 'ctx', 'sub'), 'head'), parts along dimension 0, may hold values from -40 to 40
- q_weight: bfloat16 [3584, 3584], P('sub', 'head'), may hold values from -0.09375 to 0.09375
- k_weight: bfloat16 [3584, 512], P('sub', 'head'), may hold values from -0.09375 to 0.09375
- v_weight: bfloat16 [3584, 512], P('sub', 'head'), may hold values from -0.09375 to 0.09375
- q_bias: float32 [3584], P('head'), may hold values from -3 to 3
- v_bias: float32 [512], P('head'), may hold values from -3 to 3
Outputs:
- head_outputs: bfloat16 [16384, 3584], P(('groups', 'ctx', 'sub')), parts along dimension 0
The draws below stay inside these ranges and needn't reach their ends.
There are 2 independent parts, one for each index of `groups`. The reference program is written for one: setup_inputs(seed, part) draws one part's arguments, and reference() takes and returns one part's arrays. A program takes and returns all parts, laid end to end along the dimension named above; an argument that names none is the same for every part. Nothing has to cross between parts.
All inputs are finite; a program needn't handle non-finite values.
Results may differ from the reference program's by a relative error of at most 0.0059.
Values may be sent and summed in bfloat16 or wider, within the bound.
A program may use at most 128 MiB of HBM per device.

```python
import math
import jax
import jax.numpy as jnp
from jax import lax

D = 3584
HQ = 28
KVH = 4
HD = 128
BLOCK = 128
BLK_DEV = 8
WINDOW = 8192


def draw_tokens(key, part):
    first_key = jax.random.fold_in(jax.random.fold_in(key, 17), 0)
    noise = jax.random.normal(first_key, (WINDOW, D), jnp.float32)
    values = noise
    return jnp.clip(values, -40.0, 40.0).astype(jnp.bfloat16)


def steps_of(own_key, dims, cuts, smallest, top_value):
    factor_of = 1.0
    for position, parts in cuts:
        heights = jax.random.uniform(jax.random.fold_in(jax.random.fold_in(own_key, 6), position), (parts,), jnp.float32, smallest / len(cuts), top_value / len(cuts))
        factor_of = factor_of * jnp.repeat(jnp.exp(heights), dims[position] // parts).reshape((-1,) + (1,) * (len(dims) - 1 - position))
    return factor_of


def scatter_about(stream_key, shape, spread, reach, cuts=(), kind=jnp.bfloat16):
    drawn = spread * jax.random.normal(stream_key, shape, jnp.float32)
    if cuts:
        drawn = drawn * steps_of(stream_key, shape, cuts, -0.22, 0.18)
    return jnp.clip(drawn, -reach, reach).astype(kind)


def setup_inputs(seed: int = 0, part: int = 0) -> dict:
    seeds = jax.random.split(jax.random.key(seed), 7)
    own_keys = jax.random.split(jax.random.fold_in(seeds[6], part), 7)
    tokens = draw_tokens(jax.random.fold_in(jax.random.fold_in(seeds[6], part), 71), part)
    q_weight = scatter_about(seeds[1], (D, HQ * HD), D ** -0.5, 0.09375, ((0, 2), (1, 2)))
    k_weight = scatter_about(seeds[2], (D, KVH * HD), D ** -0.5, 0.09375, ((0, 2), (1, 2)))
    v_weight = scatter_about(seeds[3], (D, KVH * HD), D ** -0.5, 0.09375, ((0, 2), (1, 2)))
    q_bias = scatter_about(seeds[4], (HQ * HD,), 0.5, 3.0, ((0, 2),), jnp.float32)
    v_bias = scatter_about(seeds[5], (KVH * HD,), 0.5, 3.0, ((0, 2),), jnp.float32)
    return {"tokens": tokens, "q_weight": q_weight, "k_weight": k_weight, "v_weight": v_weight, "q_bias": q_bias, "v_bias": v_bias}


def rotate(values, positions):
    half = values.shape[-1] // 2
    freqs = jnp.exp(-(2.0 * jnp.arange(half, dtype=jnp.float32) / (2 * half)) * math.log(1000000.0))
    angle = positions[:, None] * freqs[None, :]
    cosine = jnp.cos(angle)[:, None, :]
    sine = jnp.sin(angle)[:, None, :]
    first = values[..., :half]
    second = values[..., half:]
    return jnp.concatenate([first * cosine - second * sine, second * cosine + first * sine], axis=-1)

def reference(tokens, q_weight, k_weight, v_weight, q_bias, v_bias):
    group = HQ // KVH
    nblocks = WINDOW // BLOCK
    positions = jnp.arange(WINDOW, dtype=jnp.float32)
    distances = jnp.array([0, 1, 2, 4, 8, 16, 32, 64, 128], dtype=jnp.int32)
    scale = 1.0 / math.sqrt(HD)
    lower = jnp.arange(BLOCK, dtype=jnp.int32)[:, None] >= jnp.arange(BLOCK, dtype=jnp.int32)[None, :]
    notself = jnp.arange(9, dtype=jnp.int32) != 0

    def one_head(head_index):
        w_query = lax.dynamic_slice_in_dim(q_weight, head_index * group * HD, group * HD, 1)
        w_key = lax.dynamic_slice_in_dim(k_weight, head_index * HD, HD, 1)
        w_value = lax.dynamic_slice_in_dim(v_weight, head_index * HD, HD, 1)
        query = jnp.dot(tokens, w_query, preferred_element_type=jnp.float32) + lax.dynamic_slice_in_dim(q_bias, head_index * group * HD, group * HD, 0)
        keyed = jnp.dot(tokens, w_key, preferred_element_type=jnp.float32)
        valued = jnp.dot(tokens, w_value, preferred_element_type=jnp.float32) + lax.dynamic_slice_in_dim(v_bias, head_index * HD, HD, 0)
        query = rotate(query.reshape(WINDOW, group, HD), positions).astype(jnp.bfloat16)
        keyed = rotate(keyed.reshape(WINDOW, 1, HD), positions).astype(jnp.bfloat16)
        valued = valued.astype(jnp.bfloat16)
        key_blocks = keyed.reshape(nblocks, BLOCK, HD)
        value_blocks = valued.reshape(nblocks, BLOCK, HD)
        query_blocks = query.reshape(nblocks, BLOCK, group, HD)

        def one_group(start):
            global_block = start + jnp.arange(BLK_DEV, dtype=jnp.int32)
            query_group = lax.dynamic_slice_in_dim(query_blocks, start, BLK_DEV, 0)
            index = global_block[:, None] - distances[None, :]
            valid = index >= 0
            clipped = jnp.maximum(index, 0).astype(jnp.int32)
            keys = key_blocks[clipped].reshape(BLK_DEV, 9 * BLOCK, HD)
            vals = value_blocks[clipped].reshape(BLK_DEV, 9 * BLOCK, HD)
            mask = valid[:, None, :, None] & (notself[None, None, :, None] | lower[None, :, None, :])
            mask = mask.reshape(BLK_DEV, BLOCK, 9 * BLOCK)
            scores = jnp.einsum('bqgd,bsd->bgqs', query_group.astype(jnp.float32), keys.astype(jnp.float32)) * scale
            scores = jnp.where(mask[:, None], scores, -1e+30)
            peak = lax.optimization_barrier(jnp.max(scores, axis=-1, keepdims=True))
            expo = jnp.exp(scores - peak)
            weights = (expo / lax.optimization_barrier(jnp.sum(expo, axis=-1, keepdims=True))).astype(jnp.bfloat16)
            return jnp.einsum('bgqs,bsd->bqgd', weights.astype(jnp.float32), vals.astype(jnp.float32)).astype(jnp.bfloat16)
        starts = jnp.arange(0, nblocks, BLK_DEV, dtype=jnp.int32)
        result = lax.map(one_group, starts)
        return result.reshape(WINDOW, group * HD)
    every = lax.map(one_head, jnp.arange(KVH, dtype=jnp.int32))
    return jnp.transpose(every, (1, 0, 2)).reshape(WINDOW, HQ * HD)
```

```python
import functools
import math

import jax
import jax.numpy as jnp
from jax import lax
from jax.experimental import pallas as pl
from jax.experimental.pallas import tpu as pltpu
from jax.sharding import PartitionSpec as P

HQ = 28
KVH = 4
HD = 128
BLOCK = 128
DISTANCES = (0, 1, 2, 4, 8, 16, 32, 64, 128)
MESH = pl.DeviceIdType.MESH
PAIR = 2


def angle_tables(my_shard, rows):
    half = HD // 2
    freqs = jnp.exp(-(2.0 * jnp.arange(half, dtype=jnp.float32) / (2 * half)) * math.log(1000000.0))
    starts = my_shard * rows + BLOCK * jnp.arange(rows // BLOCK, dtype=jnp.int32)
    points = jnp.concatenate([starts, jnp.arange(BLOCK, dtype=jnp.int32)]).astype(jnp.float32)
    angle = points[:, None] * freqs[None, :]
    cosine, sine = jnp.cos(angle), jnp.sin(angle)
    return jnp.concatenate([cosine, cosine], axis=1), jnp.concatenate([sine, sine], axis=1)


def kernel(
    sizes, tok_ref, wq_ref, wk_ref, wv_ref, qb_ref, vb_ref, cos_ref, sin_ref, out_ref,
    tok, weight, query, kv, staged, kcat, vcat,
    w_load, t_load, w_send, w_recv, t_send, t_recv, kv_send, kv_recv, o_store, o_send, o_recv,
):
    n_ctx, n_head, n_sub = sizes
    n_shards = n_ctx * n_sub
    rows, feats = tok_ref.shape
    w_rows, q_cols = wq_ref.shape
    kv_cols = wk_ref.shape[1]
    hl = kv_cols // HD
    group = HQ // KVH
    nb = rows // BLOCK
    pairs = nb // PAIR
    part = PAIR * BLOCK
    me_x = lax.axis_index("head")
    me_s = lax.axis_index("sub")
    shard = lax.axis_index("ctx") * n_sub + me_s
    near = [d for d in DISTANCES if 0 < d < nb]
    far = [d // nb for d in DISTANCES if d >= nb and d // nb < n_shards]

    def shard_id(step):
        target = lax.rem(shard + step + n_shards, n_shards)
        return {"ctx": target // n_sub, "sub": lax.rem(target, n_sub)}

    def head_id(step):
        return {"head": lax.rem(me_x + step, n_head)}

    def sub_id(step):
        return {"sub": lax.rem(me_s + step, n_sub)}

    barrier = pltpu.get_barrier_semaphore()
    for step in range(1, n_head):
        pl.semaphore_signal(barrier, inc=1, device_id=head_id(step), device_id_type=MESH)
    for step in range(1, n_sub):
        pl.semaphore_signal(barrier, inc=1, device_id=sub_id(step), device_id_type=MESH)
    for step in far:
        pl.semaphore_signal(barrier, inc=1, device_id=shard_id(-step), device_id_type=MESH)

    mine = pl.ds(pl.multiple_of(me_s * w_rows, w_rows), w_rows)
    sources = (
        (wk_ref, pl.ds(q_cols, kv_cols)),
        (wv_ref, pl.ds(q_cols + kv_cols, kv_cols)),
        (wq_ref, pl.ds(0, q_cols)),
    )
    w_loads = [
        pltpu.make_async_copy(ref, weight.at[mine, cols], w_load.at[i])
        for i, (ref, cols) in enumerate(sources)
    ]
    t_own = pltpu.make_async_copy(tok_ref, tok.at[me_x], t_load)
    for copy in w_loads:
        copy.start()
    t_own.start()
    pl.semaphore_wait(barrier, n_head - 1 + n_sub - 1 + len(far))

    def token_copy(step, c):
        piece = pl.ds(pl.multiple_of(c * part, part), part)
        return pltpu.make_async_remote_copy(
            src_ref=tok_ref.at[piece], dst_ref=tok.at[me_x, piece],
            send_sem=t_send.at[step - 1, c], recv_sem=t_recv.at[step - 1, c],
            device_id=head_id(step), device_id_type=MESH,
        )

    def weight_copy(step, i):
        ref, cols = sources[i]
        return pltpu.make_async_remote_copy(
            src_ref=ref, dst_ref=weight.at[mine, cols],
            send_sem=w_send.at[step - 1, i], recv_sem=w_recv.at[step - 1, i],
            device_id=sub_id(step), device_id_type=MESH,
        )

    for c in range(pairs):
        for step in range(1, n_head):
            token_copy(step, c).start()
        if c == 0:
            for i in range(len(sources)):
                for step in range(1, n_sub):
                    weight_copy(step, i).start()

    def kv_copy(i, c):
        return pltpu.make_async_remote_copy(
            src_ref=kv.at[0, pl.ds(c * PAIR, PAIR)],
            dst_ref=kv.at[i + 1, pl.ds(c * PAIR, PAIR)],
            send_sem=kv_send.at[i, c], recv_sem=kv_recv.at[i, c],
            device_id=shard_id(far[i]), device_id_type=MESH,
        )

    vcat[:, HD:] = jnp.ones((vcat.shape[0], HD), vcat.dtype)
    sign = jnp.where(lax.broadcasted_iota(jnp.int32, (1, HD), 1) < HD // 2, -1.0, 1.0)

    def project(c, cols):
        piece = pl.ds(pl.multiple_of(c * part, part), part)
        total = None
        for h in range(n_head):
            term = jnp.dot(
                tok[h, piece, :], weight[h * feats:(h + 1) * feats, cols],
                preferred_element_type=jnp.float32,
            )
            total = term if total is None else total + term
        return total

    def angles(c):
        found = []
        for b in range(PAIR):
            cb, sb = cos_ref[pl.ds(c * PAIR + b, 1), :], sin_ref[pl.ds(c * PAIR + b, 1), :]
            cr, sr = cos_ref[nb:, :], sin_ref[nb:, :]
            found.append((cb * cr - sb * sr, (sb * cr + cb * sr) * sign))
        return found

    def rotated(value, angle):
        return (value * angle[0] + pltpu.roll(value, HD // 2, 1) * angle[1]).astype(jnp.bfloat16)

    tile = 2 * HD if q_cols % (2 * HD) == 0 else HD

    def project_part(c):
        for step in range(1, n_head):
            token_copy(step, c).wait_recv()
        angle = angles(c)
        made = project(c, pl.ds(q_cols, 2 * kv_cols))
        for b in range(PAIR):
            lines = slice(b * BLOCK, (b + 1) * BLOCK)
            for g in range(hl):
                kv[0, c * PAIR + b, g] = rotated(made[lines, g * HD:(g + 1) * HD], angle[b])
                cols = slice(g * HD, (g + 1) * HD)
                moved = made[lines, kv_cols + g * HD:kv_cols + (g + 1) * HD] + vb_ref[:, cols]
                kv[0, c * PAIR + b, hl + g] = moved.astype(jnp.bfloat16)
        for i in range(len(far)):
            kv_copy(i, c).start()

        def columns(t, carry):
            cols = pl.ds(pl.multiple_of(t * tile, tile), tile)
            value = project(c, cols) + qb_ref[:, cols]
            for b in range(PAIR):
                for u in range(tile // HD):
                    query[c * PAIR + b, t * (tile // HD) + u] = rotated(
                        value[b * BLOCK:(b + 1) * BLOCK, u * HD:(u + 1) * HD], angle[b]
                    )
            return carry

        lax.fori_loop(0, q_cols // tile, columns, 0)

    scale = math.log2(math.e) / math.sqrt(HD)
    lower = lax.broadcasted_iota(jnp.int32, (BLOCK, BLOCK), 0) >= lax.broadcasted_iota(
        jnp.int32, (BLOCK, BLOCK), 1
    )

    def out_copies(j):
        lines = pl.ds(pl.multiple_of(j * BLOCK, BLOCK), BLOCK)
        place = out_ref.at[lines, pl.ds(pl.multiple_of(me_x * q_cols, HD), q_cols)]
        local = pltpu.make_async_copy(staged.at[lines], place, o_store.at[j])
        sends = [
            pltpu.make_async_remote_copy(
                src_ref=staged.at[lines], dst_ref=place,
                send_sem=o_send.at[step - 1, j], recv_sem=o_recv.at[step - 1, j],
                device_id=head_id(step), device_id_type=MESH,
            )
            for step in range(1, n_head)
        ]
        return local, sends

    def attend_block(j):
        slots = [(0, j, None)]
        for d in near:
            inside = j >= d
            slots.append((jnp.where(inside, 0, 1), lax.rem(j - d + nb, nb), inside | (shard >= 1)))
        for i, step in enumerate(far):
            slots.append((i + 1, j, shard >= step))
        bias = [None if ok is None else jnp.where(ok, 0.0, -1e30) for _, _, ok in slots]
        lines = pl.ds(pl.multiple_of(j * BLOCK, BLOCK), BLOCK)

        def one_group(g, carry):
            for s, (source, block, _) in enumerate(slots):
                kcat[s * BLOCK:(s + 1) * BLOCK, :] = kv[source, block, g]
                vcat[s * BLOCK:(s + 1) * BLOCK, :HD] = kv[source, block, hl + g]
            for h in range(group):
                scores = lax.dot_general(
                    query[j, g * group + h], kcat[...], (((1,), (1,)), ((), ())),
                    preferred_element_type=jnp.float32,
                )
                pieces = []
                for s in range(len(slots)):
                    piece = scores[:, s * BLOCK:(s + 1) * BLOCK] * scale
                    pieces.append(
                        jnp.where(lower, piece, -1e30) if s == 0 else piece + bias[s]
                    )
                peak = jnp.max(functools.reduce(jnp.maximum, pieces), axis=1, keepdims=True)
                expo = jnp.concatenate(
                    [jnp.exp2(piece - peak).astype(jnp.bfloat16) for piece in pieces], axis=1
                )
                summed = jnp.dot(expo, vcat[...], preferred_element_type=jnp.float32)
                cols = pl.ds(pl.multiple_of((g * group + h) * HD, HD), HD)
                staged[lines, cols] = (summed[:, :HD] / summed[:, HD:]).astype(jnp.bfloat16)
            return carry

        lax.fori_loop(0, hl, one_group, 0)
        local, sends = out_copies(j)
        for copy in sends:
            copy.start()
        local.start()

    def attend_pair(c):
        for i in range(len(far)):
            kv_copy(i, c).wait_recv()

        def one_block(b, carry):
            attend_block(c * PAIR + b)
            return carry

        lax.fori_loop(0, PAIR, one_block, 0)

    t_own.wait()
    for copy in w_loads:
        copy.wait()
    for i in range(len(sources)):
        for step in range(1, n_sub):
            weight_copy(step, i).wait_recv()

    first = max(near) // PAIR

    def turn(i, carry):
        @pl.when(i < pairs)
        def _():
            project_part(i)

        @pl.when(i >= first)
        def _():
            attend_pair(lax.rem(i, pairs))

        return carry

    lax.fori_loop(0, pairs + first, turn, 0)

    for i in range(len(sources)):
        for step in range(1, n_sub):
            weight_copy(step, i).wait_send()
    for c in range(pairs):
        for step in range(1, n_head):
            token_copy(step, c).wait_send()
        for i in range(len(far)):
            kv_copy(i, c).wait_send()
    for j in range(nb):
        local, sends = out_copies(j)
        local.wait()
        for copy in sends:
            copy.wait()


def on_device(sizes, tokens, q_weight, k_weight, v_weight, q_bias, v_bias):
    n_ctx, n_head, n_sub = sizes
    n_shards = n_ctx * n_sub
    rows, feats = tokens.shape
    w_rows, q_cols = q_weight.shape
    kv_cols = k_weight.shape[1]
    hl = kv_cols // HD
    nb = rows // BLOCK
    pairs = nb // PAIR
    n_far = len([d for d in DISTANCES if d >= nb and d // nb < n_shards])
    n_slots = len([d for d in DISTANCES if d < nb]) + n_far
    cosine, sine = angle_tables(lax.axis_index("ctx") * n_sub + lax.axis_index("sub"), rows)
    full = w_rows * n_sub
    total = q_cols + 2 * kv_cols
    dma = pltpu.SemaphoreType.DMA
    anywhere = pl.BlockSpec(memory_space=pl.ANY)
    inside = pl.BlockSpec(memory_space=pltpu.VMEM)
    return pl.pallas_call(
        functools.partial(kernel, sizes),
        out_shape=jax.ShapeDtypeStruct((rows, q_cols * n_head), jnp.bfloat16),
        in_specs=[anywhere] * 4 + [inside] * 4,
        out_specs=anywhere,
        scratch_shapes=[
            pltpu.VMEM((n_head, rows, feats), jnp.bfloat16),
            pltpu.VMEM((full, total), jnp.bfloat16),
            pltpu.VMEM((nb, q_cols // HD, BLOCK, HD), jnp.bfloat16),
            pltpu.VMEM((n_far + 1, nb, 2 * hl, BLOCK, HD), jnp.bfloat16),
            pltpu.VMEM((rows, q_cols), jnp.bfloat16),
            pltpu.VMEM((n_slots * BLOCK, HD), jnp.bfloat16),
            pltpu.VMEM((n_slots * BLOCK, 2 * HD), jnp.bfloat16),
            dma((3,)), dma,
            dma((n_sub - 1, 3)), dma((n_sub - 1, 3)),
            dma((n_head - 1, pairs)), dma((n_head - 1, pairs)),
            dma((n_far, pairs)), dma((n_far, pairs)),
            dma((nb,)), dma((n_head - 1, nb)), dma((n_head - 1, nb)),
        ],
        compiler_params=pltpu.CompilerParams(
            collective_id=0, has_side_effects=True, vmem_limit_bytes=60 * 1024 * 1024
        ),
    )(
        tokens, q_weight, k_weight, v_weight,
        q_bias.reshape(1, -1), v_bias.reshape(1, -1), cosine, sine,
    )


def solution(mesh):
    sizes = (mesh.shape["ctx"], mesh.shape["head"], mesh.shape["sub"])
    return jax.shard_map(
        functools.partial(on_device, sizes),
        mesh=mesh,
        in_specs=(
            P(("groups", "ctx", "sub"), "head"),
            P("sub", "head"),
            P("sub", "head"),
            P("sub", "head"),
            P("head"),
            P("head"),
        ),
        out_specs=P(("groups", "ctx", "sub"), None),
        check_vma=False,
    )
```

```python
import functools
import math

import jax
import jax.numpy as jnp
from jax import lax
from jax.experimental import pallas as pl
from jax.experimental.pallas import tpu as pltpu
from jax.sharding import PartitionSpec as P

HQ = 28
KVH = 4
HD = 128
BLOCK = 128
DISTANCES = (0, 1, 2, 4, 8, 16, 32, 64, 128)
MESH = pl.DeviceIdType.MESH
PAIR = 1


def small_table(my_shard, rows, q_bias, v_bias):
    half = HD // 2
    freqs = jnp.exp(-(2.0 * jnp.arange(half, dtype=jnp.float32) / (2 * half)) * math.log(1000000.0))
    freqs = jnp.concatenate([freqs, freqs])
    starts = my_shard * rows + BLOCK * jnp.arange(rows // BLOCK, dtype=jnp.int32)
    inner = jnp.arange(BLOCK, dtype=jnp.int32).astype(jnp.float32)[:, None] * freqs[None, :]
    outer = starts.astype(jnp.float32)[:, None] * freqs[None, :]
    return jnp.concatenate([
        jnp.cos(inner), jnp.sin(inner), jnp.cos(outer), jnp.sin(outer),
        q_bias.reshape(-1, HD), v_bias.reshape(-1, HD),
    ])


def kernel(
    sizes, tok_ref, wq_ref, wk_ref, wv_ref, table, out_ref,
    tok, weight, query, kv, staged, kcat, vcat,
    w_load, t_load, w_send, w_recv, t_send, t_recv, kv_send, kv_recv, o_store, o_send, o_recv,
):
    n_ctx, n_head, n_sub = sizes
    n_shards = n_ctx * n_sub
    rows, feats = tok_ref.shape
    w_rows, q_cols = wq_ref.shape
    kv_cols = wk_ref.shape[1]
    hl = kv_cols // HD
    group = HQ // KVH
    nb = rows // BLOCK
    pairs = nb // PAIR
    part = PAIR * BLOCK
    heads = q_cols // HD
    bias_at = 2 * (BLOCK + nb)
    me_x = lax.axis_index("head")
    me_s = lax.axis_index("sub")
    shard = lax.axis_index("ctx") * n_sub + me_s
    near = [d for d in DISTANCES if 0 < d < nb]
    far = [d // nb for d in DISTANCES if d >= nb and d // nb < n_shards]

    def shard_id(step):
        target = lax.rem(shard + step + n_shards, n_shards)
        return {"ctx": target // n_sub, "sub": lax.rem(target, n_sub)}

    def head_id(step):
        return {"head": lax.rem(me_x + step, n_head)}

    def sub_id(step):
        return {"sub": lax.rem(me_s + step, n_sub)}

    barrier = pltpu.get_barrier_semaphore()
    for step in range(1, n_head):
        pl.semaphore_signal(barrier, inc=1, device_id=head_id(step), device_id_type=MESH)
    for step in range(1, n_sub):
        pl.semaphore_signal(barrier, inc=1, device_id=sub_id(step), device_id_type=MESH)
    for step in far:
        pl.semaphore_signal(barrier, inc=1, device_id=shard_id(-step), device_id_type=MESH)

    mine = pl.ds(pl.multiple_of(me_s * w_rows, w_rows), w_rows)
    sources = (
        (wk_ref, pl.ds(q_cols, kv_cols)),
        (wv_ref, pl.ds(q_cols + kv_cols, kv_cols)),
        (wq_ref, pl.ds(0, q_cols)),
    )
    w_loads = [
        pltpu.make_async_copy(ref, weight.at[mine, cols], w_load.at[i])
        for i, (ref, cols) in enumerate(sources)
    ]
    t_own = pltpu.make_async_copy(tok_ref, tok.at[me_x], t_load)
    for copy in w_loads:
        copy.start()
    t_own.start()
    pl.semaphore_wait(barrier, n_head - 1 + n_sub - 1 + len(far))

    def token_copy(step, c):
        piece = pl.ds(pl.multiple_of(c * part, part), part)
        return pltpu.make_async_remote_copy(
            src_ref=tok_ref.at[piece], dst_ref=tok.at[me_x, piece],
            send_sem=t_send.at[step - 1, c], recv_sem=t_recv.at[step - 1, c],
            device_id=head_id(step), device_id_type=MESH,
        )

    def weight_copy(step, i):
        ref, cols = sources[i]
        return pltpu.make_async_remote_copy(
            src_ref=ref, dst_ref=weight.at[mine, cols],
            send_sem=w_send.at[step - 1, i], recv_sem=w_recv.at[step - 1, i],
            device_id=sub_id(step), device_id_type=MESH,
        )

    for c in range(pairs):
        for step in range(1, n_head):
            token_copy(step, c).start()
        if c == 0:
            for i in range(len(sources)):
                for step in range(1, n_sub):
                    weight_copy(step, i).start()

    def kv_copy(i, c):
        return pltpu.make_async_remote_copy(
            src_ref=kv.at[0, pl.ds(c * PAIR, PAIR)],
            dst_ref=kv.at[i + 1, pl.ds(c * PAIR, PAIR)],
            send_sem=kv_send.at[i, c], recv_sem=kv_recv.at[i, c],
            device_id=shard_id(far[i]), device_id_type=MESH,
        )

    vcat[:, HD:] = jnp.ones((vcat.shape[0], HD), vcat.dtype)
    sign = jnp.where(lax.broadcasted_iota(jnp.int32, (1, HD), 1) < HD // 2, -1.0, 1.0)

    def project(c, cols):
        piece = pl.ds(pl.multiple_of(c * part, part), part)
        total = None
        for h in range(n_head):
            term = jnp.dot(
                tok[h, piece, :], weight[h * feats:(h + 1) * feats, cols],
                preferred_element_type=jnp.float32,
            )
            total = term if total is None else total + term
        return total

    def angles(c):
        found = []
        for b in range(PAIR):
            block = c * PAIR + b
            cb, sb = table[pl.ds(2 * BLOCK + block, 1), :], table[pl.ds(2 * BLOCK + nb + block, 1), :]
            cr, sr = table[:BLOCK, :], table[BLOCK:2 * BLOCK, :]
            found.append((cb * cr - sb * sr, (sb * cr + cb * sr) * sign))
        return found

    def rotated(value, angle):
        return (value * angle[0] + pltpu.roll(value, HD // 2, 1) * angle[1]).astype(jnp.bfloat16)

    tile = 2 * HD if q_cols % (2 * HD) == 0 else HD

    def project_part(c):
        for step in range(1, n_head):
            token_copy(step, c).wait_recv()
        angle = angles(c)
        made = project(c, pl.ds(q_cols, 2 * kv_cols))
        for b in range(PAIR):
            lines = slice(b * BLOCK, (b + 1) * BLOCK)
            for g in range(hl):
                kv[0, c * PAIR + b, g] = rotated(made[lines, g * HD:(g + 1) * HD], angle[b])
                moved = made[lines, kv_cols + g * HD:kv_cols + (g + 1) * HD] + table[pl.ds(bias_at + heads + g, 1), :]
                kv[0, c * PAIR + b, hl + g] = moved.astype(jnp.bfloat16)
        for i in range(len(far)):
            kv_copy(i, c).start()

        def columns(t, carry):
            cols = pl.ds(pl.multiple_of(t * tile, tile), tile)
            value = project(c, cols)
            for b in range(PAIR):
                for u in range(tile // HD):
                    head = t * (tile // HD) + u
                    part_value = value[b * BLOCK:(b + 1) * BLOCK, u * HD:(u + 1) * HD]
                    query[c * PAIR + b, head] = rotated(
                        part_value + table[pl.ds(bias_at + head, 1), :], angle[b]
                    )
            return carry

        @pl.when(c == 0)
        def _():
            wait_weights((2,))

        lax.fori_loop(0, q_cols // tile, columns, 0)

    scale = math.log2(math.e) / math.sqrt(HD)
    lower = lax.broadcasted_iota(jnp.int32, (BLOCK, BLOCK), 0) >= lax.broadcasted_iota(
        jnp.int32, (BLOCK, BLOCK), 1
    )

    def out_copies(j):
        lines = pl.ds(pl.multiple_of(j * BLOCK, BLOCK), BLOCK)
        place = out_ref.at[lines, pl.ds(pl.multiple_of(me_x * q_cols, HD), q_cols)]
        local = pltpu.make_async_copy(staged.at[lines], place, o_store.at[j])
        sends = [
            pltpu.make_async_remote_copy(
                src_ref=staged.at[lines], dst_ref=place,
                send_sem=o_send.at[step - 1, j], recv_sem=o_recv.at[step - 1, j],
                device_id=head_id(step), device_id_type=MESH,
            )
            for step in range(1, n_head)
        ]
        return local, sends

    def attend_block(j):
        slots = [(0, j, None)]
        for d in near:
            inside = j >= d
            slots.append((jnp.where(inside, 0, 1), lax.rem(j - d + nb, nb), inside | (shard >= 1)))
        for i, step in enumerate(far):
            slots.append((i + 1, j, shard >= step))
        bias = [None if ok is None else jnp.where(ok, 0.0, -1e30) for _, _, ok in slots]
        lines = pl.ds(pl.multiple_of(j * BLOCK, BLOCK), BLOCK)

        def one_group(g, carry):
            for s, (source, block, _) in enumerate(slots):
                kcat[s * BLOCK:(s + 1) * BLOCK, :] = kv[source, block, g]
                vcat[s * BLOCK:(s + 1) * BLOCK, :HD] = kv[source, block, hl + g]
            for h in range(group):
                scores = lax.dot_general(
                    query[j, g * group + h], kcat[...], (((1,), (1,)), ((), ())),
                    preferred_element_type=jnp.float32,
                )
                pieces = []
                for s in range(len(slots)):
                    piece = scores[:, s * BLOCK:(s + 1) * BLOCK] * scale
                    pieces.append(
                        jnp.where(lower, piece, -1e30) if s == 0 else piece + bias[s]
                    )
                peak = jnp.max(functools.reduce(jnp.maximum, pieces), axis=1, keepdims=True)
                expo = jnp.concatenate(
                    [jnp.exp2(piece - peak).astype(jnp.bfloat16) for piece in pieces], axis=1
                )
                summed = jnp.dot(expo, vcat[...], preferred_element_type=jnp.float32)
                cols = pl.ds(pl.multiple_of((g * group + h) * HD, HD), HD)
                staged[lines, cols] = (summed[:, :HD] / summed[:, HD:]).astype(jnp.bfloat16)
            return carry

        lax.fori_loop(0, hl, one_group, 0)
        local, sends = out_copies(j)
        for copy in sends:
            copy.start()
        local.start()

    def attend_pair(c):
        for i in range(len(far)):
            kv_copy(i, c).wait_recv()

        def one_block(b, carry):
            attend_block(c * PAIR + b)
            return carry

        lax.fori_loop(0, PAIR, one_block, 0)

    def wait_weights(chosen):
        for i in chosen:
            w_loads[i].wait()
            for step in range(1, n_sub):
                weight_copy(step, i).wait_recv()

    t_own.wait()
    wait_weights((0, 1))

    first = max(near) // PAIR

    def turn(i, carry):
        @pl.when(i < pairs)
        def _():
            project_part(i)

        @pl.when(i > first)
        def _():
            attend_pair(lax.rem(i - 1, pairs))

        return carry

    lax.fori_loop(0, pairs + first + 1, turn, 0)

    for i in range(len(sources)):
        for step in range(1, n_sub):
            weight_copy(step, i).wait_send()
    for c in range(pairs):
        for step in range(1, n_head):
            token_copy(step, c).wait_send()
        for i in range(len(far)):
            kv_copy(i, c).wait_send()
    for j in range(nb):
        local, sends = out_copies(j)
        local.wait()
        for copy in sends:
            copy.wait()


def on_device(sizes, tokens, q_weight, k_weight, v_weight, q_bias, v_bias):
    n_ctx, n_head, n_sub = sizes
    n_shards = n_ctx * n_sub
    rows, feats = tokens.shape
    w_rows, q_cols = q_weight.shape
    kv_cols = k_weight.shape[1]
    hl = kv_cols // HD
    nb = rows // BLOCK
    pairs = nb // PAIR
    n_far = len([d for d in DISTANCES if d >= nb and d // nb < n_shards])
    n_slots = len([d for d in DISTANCES if d < nb]) + n_far
    my_shard = lax.axis_index("ctx") * n_sub + lax.axis_index("sub")
    full = w_rows * n_sub
    total = q_cols + 2 * kv_cols
    dma = pltpu.SemaphoreType.DMA
    anywhere = pl.BlockSpec(memory_space=pl.ANY)
    inside = pl.BlockSpec(memory_space=pltpu.VMEM)
    return pl.pallas_call(
        functools.partial(kernel, sizes),
        out_shape=jax.ShapeDtypeStruct((rows, q_cols * n_head), jnp.bfloat16),
        in_specs=[anywhere] * 4 + [inside],
        out_specs=anywhere,
        scratch_shapes=[
            pltpu.VMEM((n_head, rows, feats), jnp.bfloat16),
            pltpu.VMEM((full, total), jnp.bfloat16),
            pltpu.VMEM((nb, q_cols // HD, BLOCK, HD), jnp.bfloat16),
            pltpu.VMEM((n_far + 1, nb, 2 * hl, BLOCK, HD), jnp.bfloat16),
            pltpu.VMEM((rows, q_cols), jnp.bfloat16),
            pltpu.VMEM((n_slots * BLOCK, HD), jnp.bfloat16),
            pltpu.VMEM((n_slots * BLOCK, 2 * HD), jnp.bfloat16),
            dma((3,)), dma,
            dma((n_sub - 1, 3)), dma((n_sub - 1, 3)),
            dma((n_head - 1, pairs)), dma((n_head - 1, pairs)),
            dma((n_far, pairs)), dma((n_far, pairs)),
            dma((nb,)), dma((n_head - 1, nb)), dma((n_head - 1, nb)),
        ],
        compiler_params=pltpu.CompilerParams(
            collective_id=0, has_side_effects=True, vmem_limit_bytes=60 * 1024 * 1024
        ),
    )(
        tokens, q_weight, k_weight, v_weight, small_table(my_shard, rows, q_bias, v_bias),
    )


def solution(mesh):
    sizes = (mesh.shape["ctx"], mesh.shape["head"], mesh.shape["sub"])
    return jax.shard_map(
        functools.partial(on_device, sizes),
        mesh=mesh,
        in_specs=(
            P(("groups", "ctx", "sub"), "head"),
            P("sub", "head"),
            P("sub", "head"),
            P("sub", "head"),
            P("head"),
            P("head"),
        ),
        out_specs=P(("groups", "ctx", "sub"), None),
        check_vma=False,
    )
```

```python
import functools
import math

import jax
import jax.numpy as jnp
from jax import lax
from jax.experimental import pallas as pl
from jax.experimental.pallas import tpu as pltpu
from jax.sharding import PartitionSpec as P

HQ = 28
KVH = 4
HD = 128
BLOCK = 128
DISTANCES = (0, 1, 2, 4, 8, 16, 32, 64, 128)
MESH = pl.DeviceIdType.MESH
PAIR = 1


def angle_tables(my_shard, rows):
    half = HD // 2
    place = (jnp.arange(HD, dtype=jnp.int32) % half).astype(jnp.float32)
    freqs = jnp.exp(-(2.0 * place / (2 * half)) * math.log(1000000.0))
    starts = my_shard * rows + BLOCK * jnp.arange(rows // BLOCK, dtype=jnp.int32)
    inner = jnp.arange(BLOCK, dtype=jnp.int32).astype(jnp.float32)[:, None] * freqs[None, :]
    outer = starts.astype(jnp.float32)[:, None] * freqs[None, :]
    return jnp.cos(inner), jnp.sin(inner), jnp.cos(outer), jnp.sin(outer)


def kernel(
    sizes, tok_ref, wq_ref, wk_ref, wv_ref, cos_in, sin_in, cos_at, sin_at, qb_ref, vb_ref, out_ref,
    tok, weight, query, kv, kcat, vcat,
    w_load, t_load, w_send, w_recv, t_send, t_recv, kv_send, kv_recv, o_send, o_recv,
):
    n_ctx, n_head, n_sub = sizes
    n_shards = n_ctx * n_sub
    rows, feats = tok_ref.shape
    w_rows, q_cols = wq_ref.shape
    kv_cols = wk_ref.shape[1]
    hl = kv_cols // HD
    group = HQ // KVH
    nb = rows // BLOCK
    pairs = nb // PAIR
    part = PAIR * BLOCK
    me_x = lax.axis_index("head")
    me_s = lax.axis_index("sub")
    shard = lax.axis_index("ctx") * n_sub + me_s
    near = [d for d in DISTANCES if 0 < d < nb]
    far = [d // nb for d in DISTANCES if d >= nb and d // nb < n_shards]

    def shard_id(step):
        target = lax.rem(shard + step + n_shards, n_shards)
        return {"ctx": target // n_sub, "sub": lax.rem(target, n_sub)}

    def head_id(step):
        return {"head": lax.rem(me_x + step, n_head)}

    def sub_id(step):
        return {"sub": lax.rem(me_s + step, n_sub)}

    barrier = pltpu.get_barrier_semaphore()
    for step in range(1, n_head):
        pl.semaphore_signal(barrier, inc=1, device_id=head_id(step), device_id_type=MESH)
    for step in range(1, n_sub):
        pl.semaphore_signal(barrier, inc=1, device_id=sub_id(step), device_id_type=MESH)
    for step in far:
        pl.semaphore_signal(barrier, inc=1, device_id=shard_id(-step), device_id_type=MESH)

    mine = pl.ds(pl.multiple_of(me_s * w_rows, w_rows), w_rows)
    sources = (
        (wk_ref, pl.ds(q_cols, kv_cols)),
        (wv_ref, pl.ds(q_cols + kv_cols, kv_cols)),
        (wq_ref, pl.ds(0, q_cols)),
    )
    w_loads = [
        pltpu.make_async_copy(ref, weight.at[mine, cols], w_load.at[i])
        for i, (ref, cols) in enumerate(sources)
    ]
    t_own = pltpu.make_async_copy(tok_ref, tok.at[me_x], t_load)
    for copy in w_loads:
        copy.start()
    t_own.start()
    pl.semaphore_wait(barrier, n_head - 1 + n_sub - 1 + len(far))

    def token_copy(step, c):
        piece = pl.ds(pl.multiple_of(c * part, part), part)
        return pltpu.make_async_remote_copy(
            src_ref=tok_ref.at[piece], dst_ref=tok.at[me_x, piece],
            send_sem=t_send.at[step - 1, c], recv_sem=t_recv.at[step - 1, c],
            device_id=head_id(step), device_id_type=MESH,
        )

    def weight_copy(step, i):
        ref, cols = sources[i]
        return pltpu.make_async_remote_copy(
            src_ref=ref, dst_ref=weight.at[mine, cols],
            send_sem=w_send.at[step - 1, i], recv_sem=w_recv.at[step - 1, i],
            device_id=sub_id(step), device_id_type=MESH,
        )

    for c in range(pairs):
        for step in range(1, n_head):
            token_copy(step, c).start()
        if c == 0:
            for i in range(len(sources)):
                for step in range(1, n_sub):
                    weight_copy(step, i).start()

    def kv_copy(i, c):
        return pltpu.make_async_remote_copy(
            src_ref=kv.at[0, pl.ds(c * PAIR, PAIR)],
            dst_ref=kv.at[i + 1, pl.ds(c * PAIR, PAIR)],
            send_sem=kv_send.at[i, c], recv_sem=kv_recv.at[i, c],
            device_id=shard_id(far[i]), device_id_type=MESH,
        )

    vcat[:, HD:] = jnp.ones((vcat.shape[0], HD), vcat.dtype)
    sign = jnp.where(lax.broadcasted_iota(jnp.int32, (1, HD), 1) < HD // 2, -1.0, 1.0)

    def project(c, cols):
        piece = pl.ds(pl.multiple_of(c * part, part), part)
        total = None
        for h in range(n_head):
            term = jnp.dot(
                tok[h, piece, :], weight[h * feats:(h + 1) * feats, cols],
                preferred_element_type=jnp.float32,
            )
            total = term if total is None else total + term
        return total

    def angles(c):
        found = []
        for b in range(PAIR):
            block = c * PAIR + b
            cb, sb = cos_at[pl.ds(block, 1), :], sin_at[pl.ds(block, 1), :]
            cr, sr = cos_in[...], sin_in[...]
            found.append((cb * cr - sb * sr, (sb * cr + cb * sr) * sign))
        return found

    def rotated(value, angle):
        return (value * angle[0] + pltpu.roll(value, HD // 2, 1) * angle[1]).astype(jnp.bfloat16)

    tile = 2 * HD if q_cols % (2 * HD) == 0 else HD

    def project_part(c):
        for step in range(1, n_head):
            token_copy(step, c).wait_recv()
        angle = angles(c)
        made = project(c, pl.ds(q_cols, 2 * kv_cols))
        for b in range(PAIR):
            lines = slice(b * BLOCK, (b + 1) * BLOCK)
            for g in range(hl):
                kv[0, c * PAIR + b, g] = rotated(made[lines, g * HD:(g + 1) * HD], angle[b])
                moved = made[lines, kv_cols + g * HD:kv_cols + (g + 1) * HD] + vb_ref[pl.ds(g, 1), :]
                kv[0, c * PAIR + b, hl + g] = moved.astype(jnp.bfloat16)
        for i in range(len(far)):
            kv_copy(i, c).start()

        def columns(t, carry):
            cols = pl.ds(pl.multiple_of(t * tile, tile), tile)
            value = project(c, cols)
            for b in range(PAIR):
                for u in range(tile // HD):
                    head = t * (tile // HD) + u
                    part_value = value[b * BLOCK:(b + 1) * BLOCK, u * HD:(u + 1) * HD]
                    query[c * PAIR + b, head] = rotated(
                        part_value + qb_ref[pl.ds(head, 1), :], angle[b]
                    )
            return carry

        @pl.when(c == 0)
        def _():
            wait_weights((2,))

        lax.fori_loop(0, q_cols // tile, columns, 0)

    scale = math.log2(math.e) / math.sqrt(HD)
    lower = lax.broadcasted_iota(jnp.int32, (BLOCK, BLOCK), 0) >= lax.broadcasted_iota(
        jnp.int32, (BLOCK, BLOCK), 1
    )

    def out_copies(j):
        lines = pl.ds(pl.multiple_of(j * BLOCK, BLOCK), BLOCK)
        place = out_ref.at[lines, pl.ds(pl.multiple_of(me_x * q_cols, HD), q_cols)]
        return [
            pltpu.make_async_remote_copy(
                src_ref=place, dst_ref=place,
                send_sem=o_send.at[step - 1, j], recv_sem=o_recv.at[step - 1, j],
                device_id=head_id(step), device_id_type=MESH,
            )
            for step in range(1, n_head)
        ]

    def attend_block(j):
        slots = [(0, j, None)]
        for d in near:
            inside = j >= d
            slots.append((jnp.where(inside, 0, 1), lax.rem(j - d + nb, nb), inside | (shard >= 1)))
        for i, step in enumerate(far):
            slots.append((i + 1, j, shard >= step))
        bias = [None if ok is None else jnp.where(ok, 0.0, -1e30) for _, _, ok in slots]
        lines = pl.ds(pl.multiple_of(j * BLOCK, BLOCK), BLOCK)

        def one_group(g, carry):
            for s, (source, block, _) in enumerate(slots):
                kcat[s * BLOCK:(s + 1) * BLOCK, :] = kv[source, block, g]
                vcat[s * BLOCK:(s + 1) * BLOCK, :HD] = kv[source, block, hl + g]
            for h in range(group):
                scores = lax.dot_general(
                    query[j, g * group + h], kcat[...], (((1,), (1,)), ((), ())),
                    preferred_element_type=jnp.float32,
                )
                pieces = []
                for s in range(len(slots)):
                    piece = scores[:, s * BLOCK:(s + 1) * BLOCK] * scale
                    pieces.append(
                        jnp.where(lower, piece, -1e30) if s == 0 else piece + bias[s]
                    )
                peak = jnp.max(functools.reduce(jnp.maximum, pieces), axis=1, keepdims=True)
                expo = jnp.concatenate(
                    [jnp.exp2(piece - peak).astype(jnp.bfloat16) for piece in pieces], axis=1
                )
                summed = jnp.dot(expo, vcat[...], preferred_element_type=jnp.float32)
                cols = pl.ds(pl.multiple_of(me_x * q_cols + (g * group + h) * HD, HD), HD)
                out_ref[lines, cols] = (summed[:, :HD] / summed[:, HD:]).astype(jnp.bfloat16)
            return carry

        lax.fori_loop(0, hl, one_group, 0)
        for copy in out_copies(j):
            copy.start()

    def attend_pair(c):
        for i in range(len(far)):
            kv_copy(i, c).wait_recv()

        def one_block(b, carry):
            attend_block(c * PAIR + b)
            return carry

        lax.fori_loop(0, PAIR, one_block, 0)

    def wait_weights(chosen):
        for i in chosen:
            w_loads[i].wait()
            for step in range(1, n_sub):
                weight_copy(step, i).wait_recv()

    t_own.wait()
    wait_weights((0, 1))

    first = max(near) // PAIR

    def turn(i, carry):
        @pl.when(i < pairs)
        def _():
            project_part(i)

        @pl.when(i > first)
        def _():
            attend_pair(lax.rem(i - 1, pairs))

        return carry

    lax.fori_loop(0, pairs + first + 1, turn, 0)

    for i in range(len(sources)):
        for step in range(1, n_sub):
            weight_copy(step, i).wait_send()
    for c in range(pairs):
        for step in range(1, n_head):
            token_copy(step, c).wait_send()
        for i in range(len(far)):
            kv_copy(i, c).wait_send()
    for j in range(nb):
        for copy in out_copies(j):
            copy.wait()


def on_device(sizes, tokens, q_weight, k_weight, v_weight, q_bias, v_bias):
    n_ctx, n_head, n_sub = sizes
    n_shards = n_ctx * n_sub
    rows, feats = tokens.shape
    w_rows, q_cols = q_weight.shape
    kv_cols = k_weight.shape[1]
    hl = kv_cols // HD
    nb = rows // BLOCK
    pairs = nb // PAIR
    n_far = len([d for d in DISTANCES if d >= nb and d // nb < n_shards])
    n_slots = len([d for d in DISTANCES if d < nb]) + n_far
    my_shard = lax.axis_index("ctx") * n_sub + lax.axis_index("sub")
    full = w_rows * n_sub
    total = q_cols + 2 * kv_cols
    dma = pltpu.SemaphoreType.DMA
    far_memory = pl.BlockSpec(memory_space=pltpu.HBM)
    inside = pl.BlockSpec(memory_space=pltpu.VMEM)
    return pl.pallas_call(
        functools.partial(kernel, sizes),
        out_shape=pltpu.VMEM((rows, q_cols * n_head), jnp.bfloat16),
        in_specs=[far_memory] * 4 + [inside] * 6,
        out_specs=inside,
        scratch_shapes=[
            pltpu.VMEM((n_head, rows, feats), jnp.bfloat16),
            pltpu.VMEM((full, total), jnp.bfloat16),
            pltpu.VMEM((nb, q_cols // HD, BLOCK, HD), jnp.bfloat16),
            pltpu.VMEM((n_far + 1, nb, 2 * hl, BLOCK, HD), jnp.bfloat16),
            pltpu.VMEM((n_slots * BLOCK, HD), jnp.bfloat16),
            pltpu.VMEM((n_slots * BLOCK, 2 * HD), jnp.bfloat16),
            dma((3,)), dma,
            dma((n_sub - 1, 3)), dma((n_sub - 1, 3)),
            dma((n_head - 1, pairs)), dma((n_head - 1, pairs)),
            dma((n_far, pairs)), dma((n_far, pairs)),
            dma((n_head - 1, nb)), dma((n_head - 1, nb)),
        ],
        compiler_params=pltpu.CompilerParams(
            collective_id=0, has_side_effects=True, vmem_limit_bytes=54 * 1024 * 1024
        ),
    )(
        tokens, q_weight, k_weight, v_weight, *angle_tables(my_shard, rows),
        q_bias.reshape(-1, HD), v_bias.reshape(-1, HD),
    )


def solution(mesh):
    sizes = (mesh.shape["ctx"], mesh.shape["head"], mesh.shape["sub"])
    return jax.shard_map(
        functools.partial(on_device, sizes),
        mesh=mesh,
        in_specs=(
            P(("groups", "ctx", "sub"), "head"),
            P("sub", "head"),
            P("sub", "head"),
            P("sub", "head"),
            P("head"),
            P("head"),
        ),
        out_specs=P(("groups", "ctx", "sub"), None),
        check_vma=False,
    )
```

```python
import functools
import math

import jax
import jax.numpy as jnp
from jax import lax
from jax.experimental import pallas as pl
from jax.experimental.pallas import tpu as pltpu
from jax.sharding import PartitionSpec as P

HQ = 28
KVH = 4
HD = 128
BLOCK = 128
DISTANCES = (0, 1, 2, 4, 8, 16, 32, 64, 128)
MESH = pl.DeviceIdType.MESH
PAIR = 1


def angle_tables(my_shard, rows):
    half = HD // 2
    place = (jnp.arange(HD, dtype=jnp.int32) % half).astype(jnp.float32)
    freqs = jnp.exp(-(2.0 * place / (2 * half)) * math.log(1000000.0))
    starts = my_shard * rows + BLOCK * jnp.arange(rows // BLOCK, dtype=jnp.int32)
    inner = jnp.arange(BLOCK, dtype=jnp.int32).astype(jnp.float32)[:, None] * freqs[None, :]
    outer = starts.astype(jnp.float32)[:, None] * freqs[None, :]
    return jnp.cos(inner), jnp.sin(inner), jnp.cos(outer), jnp.sin(outer)


def kernel(
    sizes, tok_ref, wq_ref, wk_ref, wv_ref, cos_in, sin_in, cos_at, sin_at, qb_ref, vb_ref, out_ref,
    tok, weight, query, kv, kcat, vcat,
    w_load, t_load, w_send, w_recv, t_send, t_recv, kv_send, kv_recv, o_send, o_recv,
):
    n_ctx, n_head, n_sub = sizes
    n_shards = n_ctx * n_sub
    rows, feats = tok_ref.shape
    w_rows, q_cols = wq_ref.shape
    kv_cols = wk_ref.shape[1]
    hl = kv_cols // HD
    group = HQ // KVH
    nb = rows // BLOCK
    pairs = nb // PAIR
    part = PAIR * BLOCK
    me_x = lax.axis_index("head")
    me_s = lax.axis_index("sub")
    shard = lax.axis_index("ctx") * n_sub + me_s
    near = [d for d in DISTANCES if 0 < d < nb]
    far = [d // nb for d in DISTANCES if d >= nb and d // nb < n_shards]

    def shard_id(step):
        target = lax.rem(shard + step + n_shards, n_shards)
        return {"ctx": target // n_sub, "sub": lax.rem(target, n_sub)}

    def head_id(step):
        return {"head": lax.rem(me_x + step, n_head)}

    def sub_id(step):
        return {"sub": lax.rem(me_s + step, n_sub)}

    barrier = pltpu.get_barrier_semaphore()
    for step in range(1, n_head):
        pl.semaphore_signal(barrier, inc=1, device_id=head_id(step), device_id_type=MESH)
    for step in range(1, n_sub):
        pl.semaphore_signal(barrier, inc=1, device_id=sub_id(step), device_id_type=MESH)
    for step in far:
        pl.semaphore_signal(barrier, inc=1, device_id=shard_id(-step), device_id_type=MESH)

    mine = pl.ds(pl.multiple_of(me_s * w_rows, w_rows), w_rows)
    sources = (
        (wk_ref, pl.ds(q_cols, kv_cols)),
        (wv_ref, pl.ds(q_cols + kv_cols, kv_cols)),
        (wq_ref, pl.ds(0, q_cols)),
    )
    w_loads = [
        pltpu.make_async_copy(ref, weight.at[mine, cols], w_load.at[i])
        for i, (ref, cols) in enumerate(sources)
    ]
    t_own = pltpu.make_async_copy(tok_ref, tok.at[me_x], t_load)
    for copy in w_loads:
        copy.start()
    t_own.start()
    pl.semaphore_wait(barrier, n_head - 1 + n_sub - 1 + len(far))

    def token_copy(step, c):
        piece = pl.ds(pl.multiple_of(c * part, part), part)
        return pltpu.make_async_remote_copy(
            src_ref=tok_ref.at[piece], dst_ref=tok.at[me_x, piece],
            send_sem=t_send.at[step - 1, c], recv_sem=t_recv.at[step - 1, c],
            device_id=head_id(step), device_id_type=MESH,
        )

    def weight_copy(step, i):
        ref, cols = sources[i]
        return pltpu.make_async_remote_copy(
            src_ref=ref, dst_ref=weight.at[mine, cols],
            send_sem=w_send.at[step - 1, i], recv_sem=w_recv.at[step - 1, i],
            device_id=sub_id(step), device_id_type=MESH,
        )

    mid = max(near)
    order, attended = [], {}
    for j in range(mid, nb):
        order += [b for b in sorted(j - d for d in [0] + near) if b not in order]
        attended[len(order)] = j
    for j in range(mid):
        attended[max(attended) + 1] = j
    turns = max(attended) + 1

    def chosen_by(i, table, otherwise):
        found = otherwise
        for at, value in table:
            found = jnp.where(i == at, value, found)
        return found

    for c in order:
        for step in range(1, n_head):
            token_copy(step, c).start()
        if c == order[0]:
            for i in range(len(sources)):
                for step in range(1, n_sub):
                    weight_copy(step, i).start()

    def kv_copy(i, c):
        return pltpu.make_async_remote_copy(
            src_ref=kv.at[0, pl.ds(c * PAIR, PAIR)],
            dst_ref=kv.at[i + 1, pl.ds(c * PAIR, PAIR)],
            send_sem=kv_send.at[i, c], recv_sem=kv_recv.at[i, c],
            device_id=shard_id(far[i]), device_id_type=MESH,
        )

    vcat[:, HD:] = jnp.ones((vcat.shape[0], HD), vcat.dtype)
    sign = jnp.where(lax.broadcasted_iota(jnp.int32, (1, HD), 1) < HD // 2, -1.0, 1.0)

    def project(c, cols):
        piece = pl.ds(pl.multiple_of(c * part, part), part)
        total = None
        for h in range(n_head):
            term = jnp.dot(
                tok[h, piece, :], weight[h * feats:(h + 1) * feats, cols],
                preferred_element_type=jnp.float32,
            )
            total = term if total is None else total + term
        return total

    def angles(c):
        found = []
        for b in range(PAIR):
            block = c * PAIR + b
            cb, sb = cos_at[pl.ds(block, 1), :], sin_at[pl.ds(block, 1), :]
            cr, sr = cos_in[...], sin_in[...]
            found.append((cb * cr - sb * sr, (sb * cr + cb * sr) * sign))
        return found

    def rotated(value, angle):
        return (value * angle[0] + pltpu.roll(value, HD // 2, 1) * angle[1]).astype(jnp.bfloat16)

    tile = 2 * HD if q_cols % (2 * HD) == 0 else HD

    def project_part(c):
        for step in range(1, n_head):
            token_copy(step, c).wait_recv()
        angle = angles(c)
        made = project(c, pl.ds(q_cols, 2 * kv_cols))
        for b in range(PAIR):
            lines = slice(b * BLOCK, (b + 1) * BLOCK)
            for g in range(hl):
                kv[0, c * PAIR + b, g] = rotated(made[lines, g * HD:(g + 1) * HD], angle[b])
                moved = made[lines, kv_cols + g * HD:kv_cols + (g + 1) * HD] + vb_ref[pl.ds(g, 1), :]
                kv[0, c * PAIR + b, hl + g] = moved.astype(jnp.bfloat16)
        for i in range(len(far)):
            kv_copy(i, c).start()

        def columns(t, carry):
            cols = pl.ds(pl.multiple_of(t * tile, tile), tile)
            value = project(c, cols)
            for b in range(PAIR):
                for u in range(tile // HD):
                    head = t * (tile // HD) + u
                    part_value = value[b * BLOCK:(b + 1) * BLOCK, u * HD:(u + 1) * HD]
                    query[c * PAIR + b, head] = rotated(
                        part_value + qb_ref[pl.ds(head, 1), :], angle[b]
                    )
            return carry

        @pl.when(c == order[0])
        def _():
            wait_weights((2,))

        lax.fori_loop(0, q_cols // tile, columns, 0)

    scale = math.log2(math.e) / math.sqrt(HD)
    lower = lax.broadcasted_iota(jnp.int32, (BLOCK, BLOCK), 0) >= lax.broadcasted_iota(
        jnp.int32, (BLOCK, BLOCK), 1
    )

    def out_copies(j, g):
        lines = pl.ds(pl.multiple_of(j * BLOCK, BLOCK), BLOCK)
        first_col = pl.multiple_of(me_x * q_cols + g * (group * HD), HD)
        place = out_ref.at[lines, pl.ds(first_col, group * HD)]
        return [
            pltpu.make_async_remote_copy(
                src_ref=place, dst_ref=place,
                send_sem=o_send.at[step - 1, j, g], recv_sem=o_recv.at[step - 1, j, g],
                device_id=head_id(step), device_id_type=MESH,
            )
            for step in range(1, n_head)
        ]

    def attend_block(j):
        slots = [(0, j, None)]
        for d in near:
            inside = j >= d
            slots.append((jnp.where(inside, 0, 1), lax.rem(j - d + nb, nb), inside | (shard >= 1)))
        for i, step in enumerate(far):
            slots.append((i + 1, j, shard >= step))
        bias = [None if ok is None else jnp.where(ok, 0.0, -1e30) for _, _, ok in slots]
        lines = pl.ds(pl.multiple_of(j * BLOCK, BLOCK), BLOCK)

        def one_group(g, carry):
            for s, (source, block, _) in enumerate(slots):
                kcat[s * BLOCK:(s + 1) * BLOCK, :] = kv[source, block, g]
                vcat[s * BLOCK:(s + 1) * BLOCK, :HD] = kv[source, block, hl + g]
            for h in range(group):
                scores = lax.dot_general(
                    query[j, g * group + h], kcat[...], (((1,), (1,)), ((), ())),
                    preferred_element_type=jnp.float32,
                )
                pieces = []
                for s in range(len(slots)):
                    piece = scores[:, s * BLOCK:(s + 1) * BLOCK] * scale
                    pieces.append(
                        jnp.where(lower, piece, -1e30) if s == 0 else piece + bias[s]
                    )
                peak = jnp.max(functools.reduce(jnp.maximum, pieces), axis=1, keepdims=True)
                expo = jnp.concatenate(
                    [jnp.exp2(piece - peak).astype(jnp.bfloat16) for piece in pieces], axis=1
                )
                summed = jnp.dot(expo, vcat[...], preferred_element_type=jnp.float32)
                cols = pl.ds(pl.multiple_of(me_x * q_cols + (g * group + h) * HD, HD), HD)
                out_ref[lines, cols] = (summed[:, :HD] / summed[:, HD:]).astype(jnp.bfloat16)
            for copy in out_copies(j, g):
                copy.start()
            return carry

        lax.fori_loop(0, hl, one_group, 0)

    def attend_ready(c):
        for i in range(len(far)):
            kv_copy(i, c).wait_recv()

        attend_block(c)

    def wait_weights(chosen):
        for i in chosen:
            w_loads[i].wait()
            for step in range(1, n_sub):
                weight_copy(step, i).wait_recv()

    t_own.wait()
    wait_weights((0, 1))

    def turn(i, carry):
        @pl.when(i < pairs)
        def _():
            project_part(chosen_by(i, list(enumerate(order)), 0))

        block = chosen_by(i, list(attended.items()), -1)

        @pl.when(block >= 0)
        def _():
            attend_ready(block)

        return carry

    lax.fori_loop(0, turns, turn, 0)

    for i in range(len(sources)):
        for step in range(1, n_sub):
            weight_copy(step, i).wait_send()
    for c in range(pairs):
        for step in range(1, n_head):
            token_copy(step, c).wait_send()
        for i in range(len(far)):
            kv_copy(i, c).wait_send()
    for j in range(nb):
        for g in range(hl):
            for copy in out_copies(j, g):
                copy.wait()


def on_device(sizes, tokens, q_weight, k_weight, v_weight, q_bias, v_bias):
    n_ctx, n_head, n_sub = sizes
    n_shards = n_ctx * n_sub
    rows, feats = tokens.shape
    w_rows, q_cols = q_weight.shape
    kv_cols = k_weight.shape[1]
    hl = kv_cols // HD
    nb = rows // BLOCK
    pairs = nb // PAIR
    n_far = len([d for d in DISTANCES if d >= nb and d // nb < n_shards])
    n_slots = len([d for d in DISTANCES if d < nb]) + n_far
    my_shard = lax.axis_index("ctx") * n_sub + lax.axis_index("sub")
    full = w_rows * n_sub
    total = q_cols + 2 * kv_cols
    dma = pltpu.SemaphoreType.DMA
    far_memory = pl.BlockSpec(memory_space=pltpu.HBM)
    inside = pl.BlockSpec(memory_space=pltpu.VMEM)
    return pl.pallas_call(
        functools.partial(kernel, sizes),
        out_shape=pltpu.VMEM((rows, q_cols * n_head), jnp.bfloat16),
        in_specs=[far_memory] * 4 + [inside] * 6,
        out_specs=inside,
        scratch_shapes=[
            pltpu.VMEM((n_head, rows, feats), jnp.bfloat16),
            pltpu.VMEM((full, total), jnp.bfloat16),
            pltpu.VMEM((nb, q_cols // HD, BLOCK, HD), jnp.bfloat16),
            pltpu.VMEM((n_far + 1, nb, 2 * hl, BLOCK, HD), jnp.bfloat16),
            pltpu.VMEM((n_slots * BLOCK, HD), jnp.bfloat16),
            pltpu.VMEM((n_slots * BLOCK, 2 * HD), jnp.bfloat16),
            dma((3,)), dma,
            dma((n_sub - 1, 3)), dma((n_sub - 1, 3)),
            dma((n_head - 1, pairs)), dma((n_head - 1, pairs)),
            dma((n_far, pairs)), dma((n_far, pairs)),
            dma((n_head - 1, nb, hl)), dma((n_head - 1, nb, hl)),
        ],
        compiler_params=pltpu.CompilerParams(
            collective_id=0, has_side_effects=True, vmem_limit_bytes=54 * 1024 * 1024
        ),
    )(
        tokens, q_weight, k_weight, v_weight, *angle_tables(my_shard, rows),
        q_bias.reshape(-1, HD), v_bias.reshape(-1, HD),
    )


def solution(mesh):
    sizes = (mesh.shape["ctx"], mesh.shape["head"], mesh.shape["sub"])
    return jax.shard_map(
        functools.partial(on_device, sizes),
        mesh=mesh,
        in_specs=(
            P(("groups", "ctx", "sub"), "head"),
            P("sub", "head"),
            P("sub", "head"),
            P("sub", "head"),
            P("head"),
            P("head"),
        ),
        out_specs=P(("groups", "ctx", "sub"), None),
        check_vma=False,
    )
```

```python
import functools
import math

import jax
import jax.numpy as jnp
from jax import lax
from jax.experimental import pallas as pl
from jax.experimental.pallas import tpu as pltpu
from jax.sharding import PartitionSpec as P

HQ = 28
KVH = 4
HD = 128
BLOCK = 128
DISTANCES = (0, 1, 2, 4, 8, 16, 32, 64, 128)
MESH = pl.DeviceIdType.MESH
PAIR = 1


def kernel(
    sizes, tok_ref, wq_ref, wk_ref, wv_ref, qb_hbm, vb_hbm, out_ref,
    qb_ref, vb_ref, cos_in, sin_in, cos_at, sin_at, tok, weight, query, kv, kcat, vcat,
    b_load, w_load, t_load, w_send, w_recv, t_send, t_recv, kv_send, kv_recv, o_send, o_recv,
):
    n_ctx, n_head, n_sub = sizes
    n_shards = n_ctx * n_sub
    rows, feats = tok_ref.shape
    w_rows, q_cols = wq_ref.shape
    kv_cols = wk_ref.shape[1]
    hl = kv_cols // HD
    group = HQ // KVH
    nb = rows // BLOCK
    pairs = nb // PAIR
    part = PAIR * BLOCK
    me_x = lax.axis_index("head")
    me_s = lax.axis_index("sub")
    shard = lax.axis_index("ctx") * n_sub + me_s
    near = [d for d in DISTANCES if 0 < d < nb]
    far = [d // nb for d in DISTANCES if d >= nb and d // nb < n_shards]

    def shard_id(step):
        target = lax.rem(shard + step + n_shards, n_shards)
        return {"ctx": target // n_sub, "sub": lax.rem(target, n_sub)}

    def head_id(step):
        return {"head": lax.rem(me_x + step, n_head)}

    def sub_id(step):
        return {"sub": lax.rem(me_s + step, n_sub)}

    barrier = pltpu.get_barrier_semaphore()
    for step in range(1, n_head):
        pl.semaphore_signal(barrier, inc=1, device_id=head_id(step), device_id_type=MESH)
    for step in range(1, n_sub):
        pl.semaphore_signal(barrier, inc=1, device_id=sub_id(step), device_id_type=MESH)
    for step in far:
        pl.semaphore_signal(barrier, inc=1, device_id=shard_id(-step), device_id_type=MESH)

    mine = pl.ds(pl.multiple_of(me_s * w_rows, w_rows), w_rows)
    sources = (
        (wk_ref, pl.ds(q_cols, kv_cols)),
        (wv_ref, pl.ds(q_cols + kv_cols, kv_cols)),
        (wq_ref, pl.ds(0, q_cols)),
    )
    w_loads = [
        pltpu.make_async_copy(ref, weight.at[mine, cols], w_load.at[i])
        for i, (ref, cols) in enumerate(sources)
    ]
    t_own = pltpu.make_async_copy(tok_ref, tok.at[me_x], t_load)
    biases = [
        pltpu.make_async_copy(qb_hbm, qb_ref, b_load.at[0]),
        pltpu.make_async_copy(vb_hbm, vb_ref, b_load.at[1]),
    ]
    pl.semaphore_wait(barrier, n_head - 1 + n_sub - 1 + len(far))

    def token_copy(step, c):
        piece = pl.ds(pl.multiple_of(c * part, part), part)
        return pltpu.make_async_remote_copy(
            src_ref=tok_ref.at[piece], dst_ref=tok.at[me_x, piece],
            send_sem=t_send.at[step - 1, c], recv_sem=t_recv.at[step - 1, c],
            device_id=head_id(step), device_id_type=MESH,
        )

    def weight_copy(step, i):
        ref, cols = sources[i]
        return pltpu.make_async_remote_copy(
            src_ref=ref, dst_ref=weight.at[mine, cols],
            send_sem=w_send.at[step - 1, i], recv_sem=w_recv.at[step - 1, i],
            device_id=sub_id(step), device_id_type=MESH,
        )

    mid = max(near)
    order, attended = [], {}
    for j in range(mid, nb):
        order += [b for b in sorted(j - d for d in [0] + near) if b not in order]
        attended[len(order)] = j
    for j in range(mid):
        attended[max(attended) + 1] = j
    turns = max(attended) + 1

    def chosen_by(i, table, otherwise):
        found = otherwise
        for at, value in table:
            found = jnp.where(i == at, value, found)
        return found

    for c in order:
        for step in range(1, n_head):
            token_copy(step, c).start()
        if c == order[0]:
            for i in range(len(sources)):
                for step in range(1, n_sub):
                    weight_copy(step, i).start()

    for copy in w_loads + [t_own] + biases:
        copy.start()

    def kv_copy(i, c):
        return pltpu.make_async_remote_copy(
            src_ref=kv.at[0, pl.ds(c * PAIR, PAIR)],
            dst_ref=kv.at[i + 1, pl.ds(c * PAIR, PAIR)],
            send_sem=kv_send.at[i, c], recv_sem=kv_recv.at[i, c],
            device_id=shard_id(far[i]), device_id_type=MESH,
        )

    vcat[:, HD:] = jnp.ones((vcat.shape[0], HD), vcat.dtype)
    lane = lax.broadcasted_iota(jnp.int32, (1, HD), 1) % (HD // 2)
    freqs = jnp.exp(-(2.0 * lane.astype(jnp.float32) / HD) * math.log(1000000.0))
    inner = lax.broadcasted_iota(jnp.int32, (BLOCK, HD), 0).astype(jnp.float32) * freqs
    cos_in[...], sin_in[...] = jnp.cos(inner), jnp.sin(inner)
    starts = shard * rows + BLOCK * lax.broadcasted_iota(jnp.int32, (nb, HD), 0)
    outer = starts.astype(jnp.float32) * freqs
    cos_at[...], sin_at[...] = jnp.cos(outer), jnp.sin(outer)
    sign = jnp.where(lax.broadcasted_iota(jnp.int32, (1, HD), 1) < HD // 2, -1.0, 1.0)

    def project(c, cols):
        piece = pl.ds(pl.multiple_of(c * part, part), part)
        total = None
        for h in range(n_head):
            term = jnp.dot(
                tok[h, piece, :], weight[h * feats:(h + 1) * feats, cols],
                preferred_element_type=jnp.float32,
            )
            total = term if total is None else total + term
        return total

    def angles(c):
        found = []
        for b in range(PAIR):
            block = c * PAIR + b
            cb, sb = cos_at[pl.ds(block, 1), :], sin_at[pl.ds(block, 1), :]
            cr, sr = cos_in[...], sin_in[...]
            found.append((cb * cr - sb * sr, (sb * cr + cb * sr) * sign))
        return found

    def rotated(value, angle):
        return (value * angle[0] + pltpu.roll(value, HD // 2, 1) * angle[1]).astype(jnp.bfloat16)

    tile = 2 * HD if q_cols % (2 * HD) == 0 else HD

    def project_part(c):
        for step in range(1, n_head):
            token_copy(step, c).wait_recv()
        angle = angles(c)
        made = project(c, pl.ds(q_cols, 2 * kv_cols))
        for b in range(PAIR):
            lines = slice(b * BLOCK, (b + 1) * BLOCK)
            for g in range(hl):
                kv[0, c * PAIR + b, g] = rotated(made[lines, g * HD:(g + 1) * HD], angle[b])
                moved = made[lines, kv_cols + g * HD:kv_cols + (g + 1) * HD] + vb_ref[pl.ds(g, 1), :]
                kv[0, c * PAIR + b, hl + g] = moved.astype(jnp.bfloat16)
        for i in range(len(far)):
            kv_copy(i, c).start()

        def columns(t, carry):
            cols = pl.ds(pl.multiple_of(t * tile, tile), tile)
            value = project(c, cols)
            for b in range(PAIR):
                for u in range(tile // HD):
                    head = t * (tile // HD) + u
                    part_value = value[b * BLOCK:(b + 1) * BLOCK, u * HD:(u + 1) * HD]
                    query[c * PAIR + b, head] = rotated(
                        part_value + qb_ref[pl.ds(head, 1), :], angle[b]
                    )
            return carry

        @pl.when(c == order[0])
        def _():
            wait_weights((2,))

        lax.fori_loop(0, q_cols // tile, columns, 0)

    scale = math.log2(math.e) / math.sqrt(HD)
    lower = lax.broadcasted_iota(jnp.int32, (BLOCK, BLOCK), 0) >= lax.broadcasted_iota(
        jnp.int32, (BLOCK, BLOCK), 1
    )

    def out_copies(j, g):
        lines = pl.ds(pl.multiple_of(j * BLOCK, BLOCK), BLOCK)
        first_col = pl.multiple_of(me_x * q_cols + g * (group * HD), HD)
        place = out_ref.at[lines, pl.ds(first_col, group * HD)]
        return [
            pltpu.make_async_remote_copy(
                src_ref=place, dst_ref=place,
                send_sem=o_send.at[step - 1, j, g], recv_sem=o_recv.at[step - 1, j, g],
                device_id=head_id(step), device_id_type=MESH,
            )
            for step in range(1, n_head)
        ]

    def attend_block(j):
        slots = [(0, j, None)]
        for d in near:
            inside = j >= d
            slots.append((jnp.where(inside, 0, 1), lax.rem(j - d + nb, nb), inside | (shard >= 1)))
        for i, step in enumerate(far):
            slots.append((i + 1, j, shard >= step))
        bias = [None if ok is None else jnp.where(ok, 0.0, -1e30) for _, _, ok in slots]
        lines = pl.ds(pl.multiple_of(j * BLOCK, BLOCK), BLOCK)

        def one_group(g, carry):
            for s, (source, block, _) in enumerate(slots):
                kcat[s * BLOCK:(s + 1) * BLOCK, :] = kv[source, block, g]
                vcat[s * BLOCK:(s + 1) * BLOCK, :HD] = kv[source, block, hl + g]
            for h in range(group):
                scores = lax.dot_general(
                    query[j, g * group + h], kcat[...], (((1,), (1,)), ((), ())),
                    preferred_element_type=jnp.float32,
                )
                pieces = []
                for s in range(len(slots)):
                    piece = scores[:, s * BLOCK:(s + 1) * BLOCK] * scale
                    pieces.append(
                        jnp.where(lower, piece, -1e30) if s == 0 else piece + bias[s]
                    )
                peak = jnp.max(functools.reduce(jnp.maximum, pieces), axis=1, keepdims=True)
                expo = jnp.concatenate(
                    [jnp.exp2(piece - peak).astype(jnp.bfloat16) for piece in pieces], axis=1
                )
                summed = jnp.dot(expo, vcat[...], preferred_element_type=jnp.float32)
                cols = pl.ds(pl.multiple_of(me_x * q_cols + (g * group + h) * HD, HD), HD)
                out_ref[lines, cols] = (summed[:, :HD] / summed[:, HD:]).astype(jnp.bfloat16)
            for copy in out_copies(j, g):
                copy.start()
            return carry

        lax.fori_loop(0, hl, one_group, 0)

    def attend_ready(c):
        for i in range(len(far)):
            kv_copy(i, c).wait_recv()

        attend_block(c)

    def wait_weights(chosen):
        for i in chosen:
            w_loads[i].wait()
            for step in range(1, n_sub):
                weight_copy(step, i).wait_recv()

    for copy in biases:
        copy.wait()
    t_own.wait()
    wait_weights((0, 1))

    def turn(i, carry):
        @pl.when(i < pairs)
        def _():
            project_part(chosen_by(i, list(enumerate(order)), 0))

        block = chosen_by(i, list(attended.items()), -1)

        @pl.when(block >= 0)
        def _():
            attend_ready(block)

        return carry

    lax.fori_loop(0, turns, turn, 0)

    for i in range(len(sources)):
        for step in range(1, n_sub):
            weight_copy(step, i).wait_send()
    for c in range(pairs):
        for step in range(1, n_head):
            token_copy(step, c).wait_send()
        for i in range(len(far)):
            kv_copy(i, c).wait_send()
    for j in range(nb):
        for g in range(hl):
            for copy in out_copies(j, g):
                copy.wait()


def on_device(sizes, tokens, q_weight, k_weight, v_weight, q_bias, v_bias):
    n_ctx, n_head, n_sub = sizes
    n_shards = n_ctx * n_sub
    rows, feats = tokens.shape
    w_rows, q_cols = q_weight.shape
    kv_cols = k_weight.shape[1]
    hl = kv_cols // HD
    nb = rows // BLOCK
    pairs = nb // PAIR
    n_far = len([d for d in DISTANCES if d >= nb and d // nb < n_shards])
    n_slots = len([d for d in DISTANCES if d < nb]) + n_far
    full = w_rows * n_sub
    total = q_cols + 2 * kv_cols
    dma = pltpu.SemaphoreType.DMA
    far_memory = pl.BlockSpec(memory_space=pltpu.HBM)
    inside = pl.BlockSpec(memory_space=pltpu.VMEM)
    return pl.pallas_call(
        functools.partial(kernel, sizes),
        out_shape=pltpu.VMEM((rows, q_cols * n_head), jnp.bfloat16),
        in_specs=[far_memory] * 6,
        out_specs=inside,
        scratch_shapes=[
            pltpu.VMEM((q_cols // HD, HD), jnp.float32),
            pltpu.VMEM((hl, HD), jnp.float32),
            pltpu.VMEM((BLOCK, HD), jnp.float32),
            pltpu.VMEM((BLOCK, HD), jnp.float32),
            pltpu.VMEM((nb, HD), jnp.float32),
            pltpu.VMEM((nb, HD), jnp.float32),
            pltpu.VMEM((n_head, rows, feats), jnp.bfloat16),
            pltpu.VMEM((full, total), jnp.bfloat16),
            pltpu.VMEM((nb, q_cols // HD, BLOCK, HD), jnp.bfloat16),
            pltpu.VMEM((n_far + 1, nb, 2 * hl, BLOCK, HD), jnp.bfloat16),
            pltpu.VMEM((n_slots * BLOCK, HD), jnp.bfloat16),
            pltpu.VMEM((n_slots * BLOCK, 2 * HD), jnp.bfloat16),
            dma((2,)), dma((3,)), dma,
            dma((n_sub - 1, 3)), dma((n_sub - 1, 3)),
            dma((n_head - 1, pairs)), dma((n_head - 1, pairs)),
            dma((n_far, pairs)), dma((n_far, pairs)),
            dma((n_head - 1, nb, hl)), dma((n_head - 1, nb, hl)),
        ],
        compiler_params=pltpu.CompilerParams(
            collective_id=0, has_side_effects=True, vmem_limit_bytes=54 * 1024 * 1024
        ),
    )(
        tokens, q_weight, k_weight, v_weight,
        q_bias.reshape(-1, HD), v_bias.reshape(-1, HD),
    )


def solution(mesh):
    sizes = (mesh.shape["ctx"], mesh.shape["head"], mesh.shape["sub"])
    return jax.shard_map(
        functools.partial(on_device, sizes),
        mesh=mesh,
        in_specs=(
            P(("groups", "ctx", "sub"), "head"),
            P("sub", "head"),
            P("sub", "head"),
            P("sub", "head"),
            P("head"),
            P("head"),
        ),
        out_specs=P(("groups", "ctx", "sub"), None),
        check_vma=False,
    )
```

```python
import functools
import math

import jax
import jax.numpy as jnp
from jax import lax
from jax.experimental import pallas as pl
from jax.experimental.pallas import tpu as pltpu
from jax.sharding import PartitionSpec as P

HQ = 28
KVH = 4
HD = 128
BLOCK = 128
DISTANCES = (0, 1, 2, 4, 8, 16, 32, 64, 128)
MESH = pl.DeviceIdType.MESH
PAIR = 1


def kernel(
    sizes, tok_ref, wq_ref, wk_ref, wv_ref, qb_hbm, vb_hbm, out_ref,
    qb_ref, vb_ref, cos_in, sin_in, cos_at, sin_at, tok, weight, query, kv, kcat, vcat,
    b_load, w_load, t_load, w_send, w_recv, t_send, t_recv, kv_send, kv_recv, o_send, o_recv,
):
    n_ctx, n_head, n_sub = sizes
    n_shards = n_ctx * n_sub
    rows, feats = tok_ref.shape
    w_rows, q_cols = wq_ref.shape
    kv_cols = wk_ref.shape[1]
    hl = kv_cols // HD
    group = HQ // KVH
    nb = rows // BLOCK
    pairs = nb // PAIR
    part = PAIR * BLOCK
    me_x = lax.axis_index("head")
    me_s = lax.axis_index("sub")
    shard = lax.axis_index("ctx") * n_sub + me_s
    near = [d for d in DISTANCES if 0 < d < nb]
    far = [d // nb for d in DISTANCES if d >= nb and d // nb < n_shards]

    def shard_id(step):
        target = lax.rem(shard + step + n_shards, n_shards)
        return {"ctx": target // n_sub, "sub": lax.rem(target, n_sub)}

    def head_id(step):
        return {"head": lax.rem(me_x + step, n_head)}

    def sub_id(step):
        return {"sub": lax.rem(me_s + step, n_sub)}

    barrier = pltpu.get_barrier_semaphore()
    for step in range(1, n_head):
        pl.semaphore_signal(barrier, inc=1, device_id=head_id(step), device_id_type=MESH)
    for step in range(1, n_sub):
        pl.semaphore_signal(barrier, inc=1, device_id=sub_id(step), device_id_type=MESH)
    for step in far:
        pl.semaphore_signal(barrier, inc=1, device_id=shard_id(-step), device_id_type=MESH)

    mine = pl.ds(pl.multiple_of(me_s * w_rows, w_rows), w_rows)
    sources = (
        (wk_ref, pl.ds(q_cols, kv_cols)),
        (wv_ref, pl.ds(q_cols + kv_cols, kv_cols)),
        (wq_ref, pl.ds(0, q_cols)),
    )
    w_loads = [
        pltpu.make_async_copy(ref, weight.at[mine, cols], w_load.at[i])
        for i, (ref, cols) in enumerate(sources)
    ]
    t_own = pltpu.make_async_copy(tok_ref, tok.at[me_x], t_load)
    biases = [
        pltpu.make_async_copy(qb_hbm, qb_ref, b_load.at[0]),
        pltpu.make_async_copy(vb_hbm, vb_ref, b_load.at[1]),
    ]
    pl.semaphore_wait(barrier, n_head - 1 + n_sub - 1 + len(far))

    def token_copy(step, c):
        piece = pl.ds(pl.multiple_of(c * part, part), part)
        return pltpu.make_async_remote_copy(
            src_ref=tok_ref.at[piece], dst_ref=tok.at[me_x, piece],
            send_sem=t_send.at[step - 1, c], recv_sem=t_recv.at[step - 1, c],
            device_id=head_id(step), device_id_type=MESH,
        )

    def weight_copy(step, i):
        ref, cols = sources[i]
        return pltpu.make_async_remote_copy(
            src_ref=ref, dst_ref=weight.at[mine, cols],
            send_sem=w_send.at[step - 1, i], recv_sem=w_recv.at[step - 1, i],
            device_id=sub_id(step), device_id_type=MESH,
        )

    mid = max(near)
    order, attended = [], {}
    for j in range(mid, nb):
        order += [b for b in sorted(j - d for d in [0] + near) if b not in order]
        attended[len(order)] = j
    for j in range(mid):
        attended[max(attended) + 1] = j
    turns = max(attended) + 1

    def chosen_by(i, table, otherwise):
        found = otherwise
        for at, value in table:
            found = jnp.where(i == at, value, found)
        return found

    for c in order:
        for step in range(1, n_head):
            token_copy(step, c).start()
        if c == order[0]:
            for i in range(len(sources)):
                for step in range(1, n_sub):
                    weight_copy(step, i).start()

    for copy in w_loads + [t_own] + biases:
        copy.start()

    def kv_copy(i, c):
        return pltpu.make_async_remote_copy(
            src_ref=kv.at[0, pl.ds(c * PAIR, PAIR)],
            dst_ref=kv.at[i + 1, pl.ds(c * PAIR, PAIR)],
            send_sem=kv_send.at[i, c], recv_sem=kv_recv.at[i, c],
            device_id=shard_id(far[i]), device_id_type=MESH,
        )

    for i, step in enumerate(far):
        @pl.when(shard < step)
        def _():
            def clear(block, carry):
                kv[i + 1, block] = jnp.zeros(kv.shape[2:], kv.dtype)
                return carry

            lax.fori_loop(0, nb, clear, 0)

    vcat[:, HD:] = jnp.ones((vcat.shape[0], HD), vcat.dtype)
    lane = lax.broadcasted_iota(jnp.int32, (1, HD), 1) % (HD // 2)
    freqs = jnp.exp(-(2.0 * lane.astype(jnp.float32) / HD) * math.log(1000000.0))
    inner = lax.broadcasted_iota(jnp.int32, (BLOCK, HD), 0).astype(jnp.float32) * freqs
    cos_in[...], sin_in[...] = jnp.cos(inner), jnp.sin(inner)
    starts = shard * rows + BLOCK * lax.broadcasted_iota(jnp.int32, (nb, HD), 0)
    outer = starts.astype(jnp.float32) * freqs
    cos_at[...], sin_at[...] = jnp.cos(outer), jnp.sin(outer)
    sign = jnp.where(lax.broadcasted_iota(jnp.int32, (1, HD), 1) < HD // 2, -1.0, 1.0)

    def project(c, cols):
        piece = pl.ds(pl.multiple_of(c * part, part), part)
        total = None
        for h in range(n_head):
            term = jnp.dot(
                tok[h, piece, :], weight[h * feats:(h + 1) * feats, cols],
                preferred_element_type=jnp.float32,
            )
            total = term if total is None else total + term
        return total

    def angles(c):
        found = []
        for b in range(PAIR):
            block = c * PAIR + b
            cb, sb = cos_at[pl.ds(block, 1), :], sin_at[pl.ds(block, 1), :]
            cr, sr = cos_in[...], sin_in[...]
            found.append((cb * cr - sb * sr, (sb * cr + cb * sr) * sign))
        return found

    def rotated(value, angle):
        return (value * angle[0] + pltpu.roll(value, HD // 2, 1) * angle[1]).astype(jnp.bfloat16)

    tile = 2 * HD if q_cols % (2 * HD) == 0 else HD

    def project_part(c):
        for step in range(1, n_head):
            token_copy(step, c).wait_recv()
        angle = angles(c)
        made = project(c, pl.ds(q_cols, 2 * kv_cols))
        for b in range(PAIR):
            lines = slice(b * BLOCK, (b + 1) * BLOCK)
            for g in range(hl):
                kv[0, c * PAIR + b, g] = rotated(made[lines, g * HD:(g + 1) * HD], angle[b])
                moved = made[lines, kv_cols + g * HD:kv_cols + (g + 1) * HD] + vb_ref[pl.ds(g, 1), :]
                kv[0, c * PAIR + b, hl + g] = moved.astype(jnp.bfloat16)
        for i, step in enumerate(far):
            @pl.when(shard + step < n_shards)
            def _():
                kv_copy(i, c).start()

        def columns(t, carry):
            cols = pl.ds(pl.multiple_of(t * tile, tile), tile)
            value = project(c, cols)
            for b in range(PAIR):
                for u in range(tile // HD):
                    head = t * (tile // HD) + u
                    part_value = value[b * BLOCK:(b + 1) * BLOCK, u * HD:(u + 1) * HD]
                    query[c * PAIR + b, head] = rotated(
                        part_value + qb_ref[pl.ds(head, 1), :], angle[b]
                    )
            return carry

        @pl.when(c == order[0])
        def _():
            wait_weights((2,))

        lax.fori_loop(0, q_cols // tile, columns, 0)

    scale = math.log2(math.e) / math.sqrt(HD)
    lower = lax.broadcasted_iota(jnp.int32, (BLOCK, BLOCK), 0) >= lax.broadcasted_iota(
        jnp.int32, (BLOCK, BLOCK), 1
    )

    def out_copies(j, g):
        lines = pl.ds(pl.multiple_of(j * BLOCK, BLOCK), BLOCK)
        first_col = pl.multiple_of(me_x * q_cols + g * (group * HD), HD)
        place = out_ref.at[lines, pl.ds(first_col, group * HD)]
        return [
            pltpu.make_async_remote_copy(
                src_ref=place, dst_ref=place,
                send_sem=o_send.at[step - 1, j, g], recv_sem=o_recv.at[step - 1, j, g],
                device_id=head_id(step), device_id_type=MESH,
            )
            for step in range(1, n_head)
        ]

    def attend_block(j):
        slots = [(0, j, None)]
        for d in near:
            inside = j >= d
            slots.append((jnp.where(inside, 0, 1), lax.rem(j - d + nb, nb), inside | (shard >= 1)))
        for i, step in enumerate(far):
            slots.append((i + 1, j, shard >= step))
        bias = [None if ok is None else jnp.where(ok, 0.0, -1e30) for _, _, ok in slots]
        lines = pl.ds(pl.multiple_of(j * BLOCK, BLOCK), BLOCK)

        def one_group(g, carry):
            for s, (source, block, _) in enumerate(slots):
                kcat[s * BLOCK:(s + 1) * BLOCK, :] = kv[source, block, g]
                vcat[s * BLOCK:(s + 1) * BLOCK, :HD] = kv[source, block, hl + g]
            for h in range(group):
                scores = lax.dot_general(
                    query[j, g * group + h], kcat[...], (((1,), (1,)), ((), ())),
                    preferred_element_type=jnp.float32,
                )
                pieces = []
                for s in range(len(slots)):
                    piece = scores[:, s * BLOCK:(s + 1) * BLOCK] * scale
                    pieces.append(
                        jnp.where(lower, piece, -1e30) if s == 0 else piece + bias[s]
                    )
                peak = jnp.max(functools.reduce(jnp.maximum, pieces), axis=1, keepdims=True)
                expo = jnp.concatenate(
                    [jnp.exp2(piece - peak).astype(jnp.bfloat16) for piece in pieces], axis=1
                )
                summed = jnp.dot(expo, vcat[...], preferred_element_type=jnp.float32)
                cols = pl.ds(pl.multiple_of(me_x * q_cols + (g * group + h) * HD, HD), HD)
                out_ref[lines, cols] = (summed[:, :HD] / summed[:, HD:]).astype(jnp.bfloat16)
            for copy in out_copies(j, g):
                copy.start()
            return carry

        lax.fori_loop(0, hl, one_group, 0)

    def attend_ready(c):
        for i, step in enumerate(far):
            @pl.when(shard >= step)
            def _():
                kv_copy(i, c).wait_recv()

        attend_block(c)

    def wait_weights(chosen):
        for i in chosen:
            w_loads[i].wait()
            for step in range(1, n_sub):
                weight_copy(step, i).wait_recv()

    for copy in biases:
        copy.wait()
    t_own.wait()
    wait_weights((0, 1))

    def turn(i, carry):
        @pl.when(i < pairs)
        def _():
            project_part(chosen_by(i, list(enumerate(order)), 0))

        block = chosen_by(i, list(attended.items()), -1)

        @pl.when(block >= 0)
        def _():
            attend_ready(block)

        return carry

    lax.fori_loop(0, turns, turn, 0)

    for i in range(len(sources)):
        for step in range(1, n_sub):
            weight_copy(step, i).wait_send()
    for c in range(pairs):
        for step in range(1, n_head):
            token_copy(step, c).wait_send()
        for i, step in enumerate(far):
            @pl.when(shard + step < n_shards)
            def _():
                kv_copy(i, c).wait_send()
    for j in range(nb):
        for g in range(hl):
            for copy in out_copies(j, g):
                copy.wait()


def on_device(sizes, tokens, q_weight, k_weight, v_weight, q_bias, v_bias):
    n_ctx, n_head, n_sub = sizes
    n_shards = n_ctx * n_sub
    rows, feats = tokens.shape
    w_rows, q_cols = q_weight.shape
    kv_cols = k_weight.shape[1]
    hl = kv_cols // HD
    nb = rows // BLOCK
    pairs = nb // PAIR
    n_far = len([d for d in DISTANCES if d >= nb and d // nb < n_shards])
    n_slots = len([d for d in DISTANCES if d < nb]) + n_far
    full = w_rows * n_sub
    total = q_cols + 2 * kv_cols
    dma = pltpu.SemaphoreType.DMA
    far_memory = pl.BlockSpec(memory_space=pltpu.HBM)
    inside = pl.BlockSpec(memory_space=pltpu.VMEM)
    return pl.pallas_call(
        functools.partial(kernel, sizes),
        out_shape=pltpu.VMEM((rows, q_cols * n_head), jnp.bfloat16),
        in_specs=[far_memory] * 6,
        out_specs=inside,
        scratch_shapes=[
            pltpu.VMEM((q_cols // HD, HD), jnp.float32),
            pltpu.VMEM((hl, HD), jnp.float32),
            pltpu.VMEM((BLOCK, HD), jnp.float32),
            pltpu.VMEM((BLOCK, HD), jnp.float32),
            pltpu.VMEM((nb, HD), jnp.float32),
            pltpu.VMEM((nb, HD), jnp.float32),
            pltpu.VMEM((n_head, rows, feats), jnp.bfloat16),
            pltpu.VMEM((full, total), jnp.bfloat16),
            pltpu.VMEM((nb, q_cols // HD, BLOCK, HD), jnp.bfloat16),
            pltpu.VMEM((n_far + 1, nb, 2 * hl, BLOCK, HD), jnp.bfloat16),
            pltpu.VMEM((n_slots * BLOCK, HD), jnp.bfloat16),
            pltpu.VMEM((n_slots * BLOCK, 2 * HD), jnp.bfloat16),
            dma((2,)), dma((3,)), dma,
            dma((n_sub - 1, 3)), dma((n_sub - 1, 3)),
            dma((n_head - 1, pairs)), dma((n_head - 1, pairs)),
            dma((n_far, pairs)), dma((n_far, pairs)),
            dma((n_head - 1, nb, hl)), dma((n_head - 1, nb, hl)),
        ],
        compiler_params=pltpu.CompilerParams(
            collective_id=0, has_side_effects=True, vmem_limit_bytes=54 * 1024 * 1024
        ),
    )(
        tokens, q_weight, k_weight, v_weight,
        q_bias.reshape(-1, HD), v_bias.reshape(-1, HD),
    )


def solution(mesh):
    sizes = (mesh.shape["ctx"], mesh.shape["head"], mesh.shape["sub"])
    return jax.shard_map(
        functools.partial(on_device, sizes),
        mesh=mesh,
        in_specs=(
            P(("groups", "ctx", "sub"), "head"),
            P("sub", "head"),
            P("sub", "head"),
            P("sub", "head"),
            P("head"),
            P("head"),
        ),
        out_specs=P(("groups", "ctx", "sub"), None),
        check_vma=False,
    )
```

```python
import functools
import math

import jax
import jax.numpy as jnp
from jax import lax
from jax.experimental import pallas as pl
from jax.experimental.pallas import tpu as pltpu
from jax.sharding import PartitionSpec as P

HQ = 28
KVH = 4
HD = 128
BLOCK = 128
DISTANCES = (0, 1, 2, 4, 8, 16, 32, 64, 128)
MESH = pl.DeviceIdType.MESH
PAIR = 1


def kernel(
    sizes, tok_ref, wq_ref, wk_ref, wv_ref, qb_hbm, vb_hbm, out_ref,
    qb_ref, vb_ref, cos_in, sin_in, cos_at, sin_at, tok, weight, query, kv, kcat, vcat,
    b_load, w_load, t_load, w_send, w_recv, t_send, t_recv, kv_send, kv_recv, o_send, o_recv,
):
    n_ctx, n_head, n_sub = sizes
    n_shards = n_ctx * n_sub
    rows, feats = tok_ref.shape
    w_rows, q_cols = wq_ref.shape
    kv_cols = wk_ref.shape[1]
    hl = kv_cols // HD
    group = HQ // KVH
    nb = rows // BLOCK
    pairs = nb // PAIR
    part = PAIR * BLOCK
    me_x = lax.axis_index("head")
    me_s = lax.axis_index("sub")
    shard = lax.axis_index("ctx") * n_sub + me_s
    near = [d for d in DISTANCES if 0 < d < nb]
    far = [d // nb for d in DISTANCES if d >= nb and d // nb < n_shards]

    def shard_id(step):
        target = lax.rem(shard + step + n_shards, n_shards)
        return {"ctx": target // n_sub, "sub": lax.rem(target, n_sub)}

    def head_id(step):
        return {"head": lax.rem(me_x + step, n_head)}

    def sub_id(step):
        return {"sub": lax.rem(me_s + step, n_sub)}

    barrier = pltpu.get_barrier_semaphore()
    for step in range(1, n_head):
        pl.semaphore_signal(barrier, inc=1, device_id=head_id(step), device_id_type=MESH)
    for step in range(1, n_sub):
        pl.semaphore_signal(barrier, inc=1, device_id=sub_id(step), device_id_type=MESH)
    for step in far:
        pl.semaphore_signal(barrier, inc=1, device_id=shard_id(-step), device_id_type=MESH)

    mine = pl.ds(pl.multiple_of(me_s * w_rows, w_rows), w_rows)
    sources = (
        (wk_ref, pl.ds(q_cols, kv_cols)),
        (wv_ref, pl.ds(q_cols + kv_cols, kv_cols)),
        (wq_ref, pl.ds(0, q_cols)),
    )
    w_loads = [
        pltpu.make_async_copy(ref, weight.at[mine, cols], w_load.at[i])
        for i, (ref, cols) in enumerate(sources)
    ]
    t_own = pltpu.make_async_copy(tok_ref, tok.at[me_x], t_load)
    biases = [
        pltpu.make_async_copy(qb_hbm, qb_ref, b_load.at[0]),
        pltpu.make_async_copy(vb_hbm, vb_ref, b_load.at[1]),
    ]
    pl.semaphore_wait(barrier, n_head - 1 + n_sub - 1 + len(far))

    def token_copy(step, c):
        piece = pl.ds(pl.multiple_of(c * part, part), part)
        return pltpu.make_async_remote_copy(
            src_ref=(tok_ref if c is order[0] else tok.at[me_x]).at[piece], dst_ref=tok.at[me_x, piece],
            send_sem=t_send.at[step - 1, c], recv_sem=t_recv.at[step - 1, c],
            device_id=head_id(step), device_id_type=MESH,
        )

    def weight_copy(step, i):
        ref, cols = sources[i]
        return pltpu.make_async_remote_copy(
            src_ref=ref, dst_ref=weight.at[mine, cols],
            send_sem=w_send.at[step - 1, i], recv_sem=w_recv.at[step - 1, i],
            device_id=sub_id(step), device_id_type=MESH,
        )

    mid = max(near)
    order, attended = [], {}
    for j in range(mid, nb):
        order += [b for b in sorted(j - d for d in [0] + near) if b not in order]
        attended[len(order)] = j
    for j in range(mid):
        attended[max(attended) + 1] = j
    turns = max(attended) + 1

    def chosen_by(i, table, otherwise):
        found = otherwise
        for at, value in table:
            found = jnp.where(i == at, value, found)
        return found

    t_own.start()
    for c in order:
        if len(order) > 1 and c == order[1]:
            t_own.wait()
        for step in range(1, n_head):
            token_copy(step, c).start()
        if c == order[0]:
            for i in range(len(sources)):
                for step in range(1, n_sub):
                    weight_copy(step, i).start()

    for copy in w_loads + biases:
        copy.start()

    def kv_copy(i, c):
        return pltpu.make_async_remote_copy(
            src_ref=kv.at[0, pl.ds(c * PAIR, PAIR)],
            dst_ref=kv.at[i + 1, pl.ds(c * PAIR, PAIR)],
            send_sem=kv_send.at[i, c], recv_sem=kv_recv.at[i, c],
            device_id=shard_id(far[i]), device_id_type=MESH,
        )

    vcat[:, HD:] = jnp.ones((vcat.shape[0], HD), vcat.dtype)
    lane = lax.broadcasted_iota(jnp.int32, (1, HD), 1) % (HD // 2)
    freqs = jnp.exp(-(2.0 * lane.astype(jnp.float32) / HD) * math.log(1000000.0))
    inner = lax.broadcasted_iota(jnp.int32, (BLOCK, HD), 0).astype(jnp.float32) * freqs
    cos_in[...], sin_in[...] = jnp.cos(inner), jnp.sin(inner)
    starts = shard * rows + BLOCK * lax.broadcasted_iota(jnp.int32, (nb, HD), 0)
    outer = starts.astype(jnp.float32) * freqs
    cos_at[...], sin_at[...] = jnp.cos(outer), jnp.sin(outer)
    sign = jnp.where(lax.broadcasted_iota(jnp.int32, (1, HD), 1) < HD // 2, -1.0, 1.0)

    def project(c, cols):
        piece = pl.ds(pl.multiple_of(c * part, part), part)
        total = None
        for h in range(n_head):
            term = jnp.dot(
                tok[h, piece, :], weight[h * feats:(h + 1) * feats, cols],
                preferred_element_type=jnp.float32,
            )
            total = term if total is None else total + term
        return total

    def angles(c):
        found = []
        for b in range(PAIR):
            block = c * PAIR + b
            cb, sb = cos_at[pl.ds(block, 1), :], sin_at[pl.ds(block, 1), :]
            cr, sr = cos_in[...], sin_in[...]
            found.append((cb * cr - sb * sr, (sb * cr + cb * sr) * sign))
        return found

    def rotated(value, angle):
        return (value * angle[0] + pltpu.roll(value, HD // 2, 1) * angle[1]).astype(jnp.bfloat16)

    tile = 2 * HD if q_cols % (2 * HD) == 0 else HD

    def project_part(c):
        for step in range(1, n_head):
            token_copy(step, c).wait_recv()
        angle = angles(c)
        made = project(c, pl.ds(q_cols, 2 * kv_cols))
        for b in range(PAIR):
            lines = slice(b * BLOCK, (b + 1) * BLOCK)
            for g in range(hl):
                kv[0, c * PAIR + b, g] = rotated(made[lines, g * HD:(g + 1) * HD], angle[b])
                moved = made[lines, kv_cols + g * HD:kv_cols + (g + 1) * HD] + vb_ref[pl.ds(g, 1), :]
                kv[0, c * PAIR + b, hl + g] = moved.astype(jnp.bfloat16)
        for i in range(len(far)):
            kv_copy(i, c).start()

        def columns(t, carry):
            cols = pl.ds(pl.multiple_of(t * tile, tile), tile)
            value = project(c, cols)
            for b in range(PAIR):
                for u in range(tile // HD):
                    head = t * (tile // HD) + u
                    part_value = value[b * BLOCK:(b + 1) * BLOCK, u * HD:(u + 1) * HD]
                    query[c * PAIR + b, head] = rotated(
                        part_value + qb_ref[pl.ds(head, 1), :], angle[b]
                    )
            return carry

        @pl.when(c == order[0])
        def _():
            wait_weights((2,))

        lax.fori_loop(0, q_cols // tile, columns, 0)

    scale = math.log2(math.e) / math.sqrt(HD)
    lower = lax.broadcasted_iota(jnp.int32, (BLOCK, BLOCK), 0) >= lax.broadcasted_iota(
        jnp.int32, (BLOCK, BLOCK), 1
    )

    def out_copies(j, g):
        lines = pl.ds(pl.multiple_of(j * BLOCK, BLOCK), BLOCK)
        first_col = pl.multiple_of(me_x * q_cols + g * (group * HD), HD)
        place = out_ref.at[lines, pl.ds(first_col, group * HD)]
        return [
            pltpu.make_async_remote_copy(
                src_ref=place, dst_ref=place,
                send_sem=o_send.at[step - 1, j, g], recv_sem=o_recv.at[step - 1, j, g],
                device_id=head_id(step), device_id_type=MESH,
            )
            for step in range(1, n_head)
        ]

    def attend_block(j):
        slots = [(0, j, None)]
        for d in near:
            inside = j >= d
            slots.append((jnp.where(inside, 0, 1), lax.rem(j - d + nb, nb), inside | (shard >= 1)))
        for i, step in enumerate(far):
            slots.append((i + 1, j, shard >= step))
        bias = [None if ok is None else jnp.where(ok, 0.0, -1e30) for _, _, ok in slots]
        lines = pl.ds(pl.multiple_of(j * BLOCK, BLOCK), BLOCK)

        def one_group(g, carry):
            for s, (source, block, _) in enumerate(slots):
                kcat[s * BLOCK:(s + 1) * BLOCK, :] = kv[source, block, g]
                vcat[s * BLOCK:(s + 1) * BLOCK, :HD] = kv[source, block, hl + g]
            for h in range(group):
                scores = lax.dot_general(
                    query[j, g * group + h], kcat[...], (((1,), (1,)), ((), ())),
                    preferred_element_type=jnp.float32,
                )
                pieces = []
                for s in range(len(slots)):
                    piece = scores[:, s * BLOCK:(s + 1) * BLOCK] * scale
                    pieces.append(
                        jnp.where(lower, piece, -1e30) if s == 0 else piece + bias[s]
                    )
                peak = jnp.max(functools.reduce(jnp.maximum, pieces), axis=1, keepdims=True)
                expo = jnp.concatenate(
                    [jnp.exp2(piece - peak).astype(jnp.bfloat16) for piece in pieces], axis=1
                )
                summed = jnp.dot(expo, vcat[...], preferred_element_type=jnp.float32)
                cols = pl.ds(pl.multiple_of(me_x * q_cols + (g * group + h) * HD, HD), HD)
                out_ref[lines, cols] = (summed[:, :HD] / summed[:, HD:]).astype(jnp.bfloat16)
            for copy in out_copies(j, g):
                copy.start()
            return carry

        lax.fori_loop(0, hl, one_group, 0)

    def attend_ready(c):
        for i in range(len(far)):
            kv_copy(i, c).wait_recv()

        attend_block(c)

    def wait_weights(chosen):
        for i in chosen:
            w_loads[i].wait()
            for step in range(1, n_sub):
                weight_copy(step, i).wait_recv()

    for copy in biases:
        copy.wait()
    wait_weights((0, 1))

    def turn(i, carry):
        @pl.when(i < pairs)
        def _():
            project_part(chosen_by(i, list(enumerate(order)), 0))

        block = chosen_by(i, list(attended.items()), -1)

        @pl.when(block >= 0)
        def _():
            attend_ready(block)

        return carry

    lax.fori_loop(0, turns, turn, 0)

    for i in range(len(sources)):
        for step in range(1, n_sub):
            weight_copy(step, i).wait_send()
    for c in range(pairs):
        for step in range(1, n_head):
            token_copy(step, c).wait_send()
        for i in range(len(far)):
            kv_copy(i, c).wait_send()
    for j in range(nb):
        for g in range(hl):
            for copy in out_copies(j, g):
                copy.wait()


def on_device(sizes, tokens, q_weight, k_weight, v_weight, q_bias, v_bias):
    n_ctx, n_head, n_sub = sizes
    n_shards = n_ctx * n_sub
    rows, feats = tokens.shape
    w_rows, q_cols = q_weight.shape
    kv_cols = k_weight.shape[1]
    hl = kv_cols // HD
    nb = rows // BLOCK
    pairs = nb // PAIR
    n_far = len([d for d in DISTANCES if d >= nb and d // nb < n_shards])
    n_slots = len([d for d in DISTANCES if d < nb]) + n_far
    full = w_rows * n_sub
    total = q_cols + 2 * kv_cols
    dma = pltpu.SemaphoreType.DMA
    far_memory = pl.BlockSpec(memory_space=pltpu.HBM)
    inside = pl.BlockSpec(memory_space=pltpu.VMEM)
    return pl.pallas_call(
        functools.partial(kernel, sizes),
        out_shape=pltpu.VMEM((rows, q_cols * n_head), jnp.bfloat16),
        in_specs=[far_memory] * 6,
        out_specs=inside,
        scratch_shapes=[
            pltpu.VMEM((q_cols // HD, HD), jnp.float32),
            pltpu.VMEM((hl, HD), jnp.float32),
            pltpu.VMEM((BLOCK, HD), jnp.float32),
            pltpu.VMEM((BLOCK, HD), jnp.float32),
            pltpu.VMEM((nb, HD), jnp.float32),
            pltpu.VMEM((nb, HD), jnp.float32),
            pltpu.VMEM((n_head, rows, feats), jnp.bfloat16),
            pltpu.VMEM((full, total), jnp.bfloat16),
            pltpu.VMEM((nb, q_cols // HD, BLOCK, HD), jnp.bfloat16),
            pltpu.VMEM((n_far + 1, nb, 2 * hl, BLOCK, HD), jnp.bfloat16),
            pltpu.VMEM((n_slots * BLOCK, HD), jnp.bfloat16),
            pltpu.VMEM((n_slots * BLOCK, 2 * HD), jnp.bfloat16),
            dma((2,)), dma((3,)), dma,
            dma((n_sub - 1, 3)), dma((n_sub - 1, 3)),
            dma((n_head - 1, pairs)), dma((n_head - 1, pairs)),
            dma((n_far, pairs)), dma((n_far, pairs)),
            dma((n_head - 1, nb, hl)), dma((n_head - 1, nb, hl)),
        ],
        compiler_params=pltpu.CompilerParams(
            collective_id=0, has_side_effects=True, vmem_limit_bytes=54 * 1024 * 1024
        ),
    )(
        tokens, q_weight, k_weight, v_weight,
        q_bias.reshape(-1, HD), v_bias.reshape(-1, HD),
    )


def solution(mesh):
    sizes = (mesh.shape["ctx"], mesh.shape["head"], mesh.shape["sub"])
    return jax.shard_map(
        functools.partial(on_device, sizes),
        mesh=mesh,
        in_specs=(
            P(("groups", "ctx", "sub"), "head"),
            P("sub", "head"),
            P("sub", "head"),
            P("sub", "head"),
            P("head"),
            P("head"),
        ),
        out_specs=P(("groups", "ctx", "sub"), None),
        check_vma=False,
    )
```
